256 devices in a mesh: role: 2 (over x_hi), dp: 4 (over y), tensor: 32 (over x_lo, z, core).
Axes of the slice: x: 4 (x_hi: 2, x_lo: 2; x = x_hi * 2 + x_lo), y: 4, z: 8, core: 2. Of those that a mesh axis runs over, the one named last changes fastest.
Arguments:
- grad_parts: bfloat16 [2, 4, 512, 2, 18432], P('role', 'dp', 'tensor'), may hold values from -18 to 18
- master: float32 [2, 512, 2, 18432], P('role', 'tensor', None, 'dp'), may hold values from -2 to 2
- moment1: float32 [2, 512, 2, 18432], P('role', 'tensor', None, 'dp'), may hold values from -6 to 6
- moment2: float32 [2, 512, 2, 18432], P('role', 'tensor', None, 'dp'), may hold values from 0.05 to 0.5
- kv_cache: bfloat16 [2, 64, 32, 256, 384], P('role', 'dp', 'tensor'), may hold values from -200 to 200
- hidden_in: bfloat16 [64, 4, 18432], P('dp', None, 'tensor'), may hold values from -60 to 60
- attn_gain: float32 [18432], replicated, may hold values from 0.1 to 1.9
- ffn_gain: float32 [18432], replicated, may hold values from 0.1 to 1.9
- lengths: int32 [64], P('dp'), may hold values from 2 to 256, as said below
Outputs:
- weights_after: float32 [2, 512, 2, 18432], P('role', 'tensor', None, 'dp')
- decoded: bfloat16 [64, 4, 18432], P('dp', None, 'tensor')
The draws below stay inside these ranges and needn't reach their ends.
Inputs may be any that keep to these rules, and one draw needn't show every extreme that they name: `lengths`: some row holds all 256 positions.
All inputs are finite; a program needn't handle non-finite values.
Results may differ from the reference program's by a relative error of at most 0.015.
Values may be sent and summed in bfloat16 or wider, within the bound.
No kernel may reach another device: no remote copies, remote signals or barrier semaphores. Data moves between devices by JAX's collectives and lax.ppermute only.
A program may use at most 128 MiB of HBM per device.

```python
import math
import jax
import jax.numpy as jnp
from jax import lax

D = 18432
QHEADS = 96
HEAD = 192
HID_DEV = 16
CTX = 256
STEPS = 4
H = 512
ROWS = 64
N_DP = 4
N_TENSOR = 32


def shared_parts(key):
    column_key = jax.random.fold_in(key, 1)
    ramp = jnp.exp(math.log(3.0) * jnp.arange(D, dtype=jnp.float32) / D)
    column_scale = ramp * jnp.exp(jax.random.uniform(column_key, (D,), jnp.float32, 0.0, math.log(2.0)))
    return column_scale


def draw_grad_parts(key, part):
    key = jax.random.fold_in(key, 5)
    noise_key = jax.random.fold_in(key, 0)
    noise = jnp.clip(jax.random.normal(noise_key, (2, N_DP, H, 2, D), jnp.float32), -4.0, 4.0)
    position = jnp.arange(N_DP, dtype=jnp.float32) / (N_DP - 1)
    shard_scale = 0.5 * jnp.exp(math.log(3.0) * position).reshape(1, N_DP, 1, 1, 1)
    values = noise * shard_scale
    return values.astype(jnp.bfloat16)


def draw_hidden_in(key, part):
    column_scale = shared_parts(key)
    key = jax.random.fold_in(key, 11)
    noise_key, row_key = jax.random.split(key)
    noise = jnp.clip(jax.random.normal(noise_key, (ROWS, STEPS, D), jnp.float32), -4.0, 4.0)
    row_scale = jnp.exp(jax.random.uniform(row_key, (ROWS, STEPS, 1), jnp.float32, math.log(0.5), math.log(2.0)))
    values = noise * column_scale[None, None, :] * row_scale
    return values.astype(jnp.bfloat16)


def draw_kv_cache(key, part):
    key = jax.random.fold_in(key, 23)
    base_key = jax.random.fold_in(key, 0)
    cache = jnp.clip(jax.random.normal(base_key, (2, ROWS, N_TENSOR, CTX, 2 * HEAD), jnp.float32), -6.0, 6.0)
    return cache.astype(jnp.bfloat16)


def draw_master(key, part):
    key = jax.random.fold_in(key, 31)
    values = jnp.clip(jax.random.normal(key, (2, H, 2, D), jnp.float32), -4.0, 4.0)
    scales = jnp.array([1.0 / math.sqrt(D), 1.0 / math.sqrt(H)], jnp.float32).reshape(1, 1, 2, 1)
    return values * scales


def draw_lengths(key, part):
    key = jax.random.fold_in(key, 47)
    value_key, spot_key = jax.random.split(key)
    drawn = jax.random.randint(value_key, (ROWS,), 2, CTX + 1, jnp.int32)
    spot = jax.random.randint(spot_key, (), 0, ROWS, jnp.int32)
    return jnp.where(jnp.arange(ROWS, dtype=jnp.int32) == spot, CTX, drawn).astype(jnp.int32)


def levels(stream_key, shape, shards, least, largest):
    level = 1.0
    for dim, shards_of in shards:
        heights = jax.random.uniform(jax.random.fold_in(jax.random.fold_in(stream_key, 6), dim), (shards_of,), jnp.float32, least / len(shards), largest / len(shards))
        level = level * jnp.repeat(jnp.exp(heights), shape[dim] // shards_of).reshape((-1,) + (1,) * (len(shape) - 1 - dim))
    return level


def centred(key, extent, scale, bound, cuts=(), kind=jnp.bfloat16):
    loudness = levels(key, extent, cuts, -0.22, 0.18) if cuts else 1.0
    result = jax.random.normal(key, extent, jnp.float32) * scale * loudness
    return jnp.minimum(jnp.maximum(result, -bound), bound).astype(kind)


def setup_inputs(seed: int = 0) -> dict:
    seeds = jax.random.split(jax.random.key(seed), 10)
    return {
        "grad_parts": draw_grad_parts(jax.random.fold_in(seeds[9], 71), 0),
        "master": draw_master(jax.random.fold_in(seeds[9], 71), 0),
        "moment1": centred(seeds[2], (2, H, 2, D), 0.5, 6.0, ((0, 2), (1, 32), (3, 4)), jnp.float32),
        "moment2": jnp.clip(jnp.exp(math.log(0.5) - 2.3025851 * jax.random.uniform(seeds[3], (2, H, 2, D), jnp.float32) ** levels(seeds[3], (2, H, 2, D), ((0, 2), (1, 32), (3, 4)), -0.2, 0.2)), 0.05, 0.5),
        "kv_cache": draw_kv_cache(jax.random.fold_in(seeds[9], 71), 0),
        "hidden_in": draw_hidden_in(jax.random.fold_in(seeds[9], 71), 0),
        "attn_gain": jnp.clip(1.0 + 0.18 * jax.random.normal(seeds[6], (D,), jnp.float32), 0.1, 1.9),
        "ffn_gain": jnp.clip(1.0 + 0.18 * jax.random.normal(seeds[7], (D,), jnp.float32), 0.1, 1.9),
        "lengths": draw_lengths(jax.random.fold_in(seeds[9], 71), 0),
    }


beta_one = 0.9
beta_two = 0.95
rate_factor = 0.5
decay_rate = 0.1
adam_eps = 1e-08
norm_eps = 1e-05
step_count = 10

def adam_update(grad_sum, weights, first, second):
    learn_rate = rate_factor / math.sqrt(D)
    first_new = beta_one * first + (1.0 - beta_one) * grad_sum
    second_new = beta_two * second + (1.0 - beta_two) * grad_sum * grad_sum
    corr_one = 1.0 - beta_one ** step_count
    corr_two = 1.0 - beta_two ** step_count
    ratio = first_new / corr_one / (jnp.sqrt(second_new / corr_two) + adam_eps)
    return weights - learn_rate * (ratio + decay_rate * weights)

def rms_scale(values, gain):
    stat = lax.optimization_barrier(jnp.sum(values * values, axis=1)) / D
    return (values * lax.rsqrt(stat + norm_eps)[:, None] * gain).astype(jnp.bfloat16)

def attend(query, keys, values, lengths, new_keys, new_values):
    scale = 1.0 / math.sqrt(HEAD)
    query_wide = query.astype(jnp.float32)
    cache_scores = jnp.einsum('rgqe,rgce->rgqc', query_wide, keys.astype(jnp.float32)) * scale
    positions = jnp.arange(keys.shape[2], dtype=jnp.int32)
    valid = positions[None, None, None, :] < lengths[:, None, None, None]
    cache_scores = jnp.where(valid, cache_scores, -jnp.inf)
    fresh_scores = jnp.einsum('rgqe,rgse->rgqs', query_wide, new_keys.astype(jnp.float32)) * scale
    top = jnp.maximum(lax.optimization_barrier(jnp.max(cache_scores, axis=3)), lax.optimization_barrier(jnp.max(fresh_scores, axis=3)))[..., None]
    cache_exp = jnp.exp(cache_scores - top)
    fresh_exp = jnp.exp(fresh_scores - top)
    total = lax.optimization_barrier(jnp.sum(cache_exp, axis=3, keepdims=True)) + lax.optimization_barrier(jnp.sum(fresh_exp, axis=3, keepdims=True))
    cache_prob = (cache_exp / total).astype(jnp.bfloat16)
    fresh_prob = (fresh_exp / total).astype(jnp.bfloat16)
    first_part = jnp.einsum('rgqc,rgce->rgqe', cache_prob.astype(jnp.float32), values.astype(jnp.float32))
    second_part = jnp.einsum('rgqs,rgse->rgqe', fresh_prob.astype(jnp.float32), new_values.astype(jnp.float32))
    return first_part + second_part

def reference(grad_parts, master, moment1, moment2, kv_cache, hidden_in, attn_gain, ffn_gain, lengths):
    grad_sum = lax.optimization_barrier(jnp.sum(grad_parts[0].astype(jnp.float32), axis=0))
    new_master = adam_update(grad_sum, master[0], moment1[0], moment2[0])
    synced = new_master.astype(jnp.bfloat16)
    weights_after = jnp.stack([new_master, synced.astype(jnp.float32)])
    up_rows = synced[:, 0, :]
    down_blocks = synced[:, 1, :].reshape(N_TENSOR, HID_DEV, D)
    per_group = QHEADS // N_TENSOR
    row_count = hidden_in.shape[0]
    keys = kv_cache[1][..., :HEAD]
    values = kv_cache[1][..., HEAD:]
    fresh_keys = []
    fresh_values = []
    outputs = []
    for step in range(STEPS):
        hidden = hidden_in[:, step, :].astype(jnp.float32)
        normed = rms_scale(hidden, attn_gain)
        query = normed.reshape(row_count, N_TENSOR, per_group, HEAD)
        fresh_keys.append(jnp.flip(query[:, :, 0, :], axis=-1))
        fresh_values.append(query[:, :, 1, :])
        attended = attend(query, keys, values, lengths, jnp.stack(fresh_keys, axis=2), jnp.stack(fresh_values, axis=2))
        middle = hidden + attended.reshape(row_count, D)
        ffn_in = rms_scale(middle, ffn_gain)
        upper = jnp.dot(ffn_in, up_rows.T, preferred_element_type=jnp.float32)
        active = jnp.square(jnp.maximum(upper, 0.0)).astype(jnp.bfloat16)
        act_blocks = active.reshape(row_count, N_TENSOR, HID_DEV).transpose(1, 0, 2)

        def add_block(running, block_pair):
            block_act, block_down = block_pair
            product = jnp.dot(block_act, block_down, preferred_element_type=jnp.float32)
            return (running + lax.optimization_barrier(product.astype(jnp.bfloat16)).astype(jnp.float32), None)
        ffn_out, unused = lax.scan(add_block, jnp.zeros((row_count, D), jnp.float32), (act_blocks, down_blocks))
        outputs.append((middle + ffn_out).astype(jnp.bfloat16))
    return (weights_after, jnp.stack(outputs, axis=1))
```

```python
import functools
import math

import jax
import jax.numpy as jnp
from jax import lax
from jax.experimental import pallas as pl
from jax.experimental.pallas import tpu as pltpu
from jax.sharding import PartitionSpec as P

D = 18432
HEAD = 192
STEPS = 4
BAND = 8


beta_one = 0.9
beta_two = 0.95
rate_factor = 0.5
decay_rate = 0.1
adam_eps = 1e-08
norm_eps = 1e-05
step_count = 10


def adam_update(grad_sum, weights, first, second):
    learn_rate = rate_factor / math.sqrt(D)
    first_new = beta_one * first + (1.0 - beta_one) * grad_sum
    second_new = beta_two * second + (1.0 - beta_two) * grad_sum * grad_sum
    corr_one = 1.0 - beta_one**step_count
    corr_two = 1.0 - beta_two**step_count
    ratio = first_new / corr_one / (jnp.sqrt(second_new / corr_two) + adam_eps)
    return weights - learn_rate * (ratio + decay_rate * weights)


def to_lanes(column, lanes):
    rows = column.shape[0]
    here = lax.broadcasted_iota(jnp.int32, (rows, lanes), 0)
    lane = lax.broadcasted_iota(jnp.int32, (rows, lanes), 1)
    return jnp.sum(jnp.where(here == lane, column, 0.0), axis=0, keepdims=True)


def to_rows(line, rows):
    lanes = line.shape[1]
    here = lax.broadcasted_iota(jnp.int32, (rows, lanes), 0)
    lane = lax.broadcasted_iota(jnp.int32, (rows, lanes), 1)
    return jnp.sum(jnp.where(here == lane, line, 0.0), axis=1, keepdims=True)


def squares_kernel(hidden_ref, out_ref):
    hidden = hidden_ref[...]
    line = to_lanes(jnp.sum(hidden * hidden, axis=1, keepdims=True), 128)
    out_ref[...] = jnp.broadcast_to(line[None], out_ref.shape)


def attend_kernel(
    pairs,
    role_ref,
    len_ref,
    hidden_ref,
    squares_ref,
    gain_ref,
    flip_gain_ref,
    flip_ref,
    out_gain_ref,
    kv_ref,
    middle_ref,
    sent_ref,
    normed_ref,
    hidden_parts_ref,
    flip_normed_ref,
):
    step = pl.program_id(0)
    groups = normed_ref.shape[0]
    rows = hidden_ref.shape[0]
    scale = 1.0 / math.sqrt(HEAD)

    @pl.when(role_ref[0] == 1)
    def _():
        @pl.when(step == 0)
        def _():
            total = jnp.sum(squares_ref[...], axis=0)[0:1]
            factor = lax.rsqrt(to_rows(total, rows) / D + norm_eps)
            hidden = hidden_ref[...]
            normed = hidden * factor * gain_ref[...]
            for q in range(groups):
                part = slice(q * HEAD, (q + 1) * HEAD)
                normed_ref[q] = normed[:, part]
                hidden_parts_ref[q] = hidden[:, part]
            flip_normed_ref[...] = flip_ref[...] * factor * flip_gain_ref[...]

        high = lax.broadcasted_iota(jnp.int32, (groups * 8, 1), 0) % 8 >= 4
        row_id = lax.broadcasted_iota(jnp.int32, (groups * 8, 8), 0) % 8
        col_id = lax.broadcasted_iota(jnp.int32, (groups * 8, 8), 1)
        fresh_ok = (row_id // 4 == col_id // 4) & (col_id % 4 <= row_id % 4)
        context = kv_ref.shape[1]
        position = lax.broadcasted_iota(jnp.int32, (groups * 8, context), 1)
        for p in range(pairs):
            pair = step * pairs + p
            first = pl.multiple_of(pair * 8, 8)
            query = jnp.concatenate(
                [normed_ref[q, pl.ds(first, 8), :] for q in range(groups)], axis=0
            ).astype(jnp.bfloat16)
            new_keys = flip_normed_ref[pl.ds(first, 8), :].astype(jnp.bfloat16)
            new_values = normed_ref[1, pl.ds(first, 8), :].astype(jnp.bfloat16)
            contract = (((1,), (1,)), ((), ()))
            scores = []
            for half in range(2):
                keys = kv_ref[2 * p + half, :, :HEAD]
                scores.append(
                    lax.dot_general(query, keys, contract, preferred_element_type=jnp.float32)
                )
            cache = jnp.where(high, scores[1], scores[0]) * scale
            length = jnp.where(high, len_ref[2 * pair + 1], len_ref[2 * pair])
            cache = jnp.where(position < length, cache, -jnp.inf)
            fresh = (
                lax.dot_general(query, new_keys, contract, preferred_element_type=jnp.float32)
                * scale
            )
            fresh = jnp.where(fresh_ok, fresh, -jnp.inf)
            top = jnp.maximum(
                jnp.max(cache, axis=1, keepdims=True), jnp.max(fresh, axis=1, keepdims=True)
            )
            cache = jnp.exp(cache - top)
            fresh = jnp.exp(fresh - top)
            total = jnp.sum(cache, axis=1, keepdims=True) + jnp.sum(fresh, axis=1, keepdims=True)
            cache = (cache / total).astype(jnp.bfloat16)
            fresh = (fresh / total).astype(jnp.bfloat16)
            weighed = []
            for half in range(2):
                values = kv_ref[2 * p + half, :, HEAD:]
                weighed.append(jnp.dot(cache, values, preferred_element_type=jnp.float32))
            attended = jnp.where(high, weighed[1], weighed[0]) + jnp.dot(
                fresh, new_values, preferred_element_type=jnp.float32
            )
            for q in range(groups):
                middle_ref[pl.ds(first, 8), q * HEAD : (q + 1) * HEAD] = (
                    hidden_parts_ref[q, pl.ds(first, 8), :] + attended[q * 8 : (q + 1) * 8]
                )

        @pl.when(step == pl.num_programs(0) - 1)
        def _():
            middle = middle_ref[...]
            width = middle.shape[1]
            squares = jnp.sum(middle * middle, axis=1, keepdims=True)
            high_part = squares.astype(jnp.bfloat16).astype(jnp.float32)
            mid_part = (squares - high_part).astype(jnp.bfloat16).astype(jnp.float32)
            low_part = squares - high_part - mid_part
            lane = lax.broadcasted_iota(jnp.int32, (rows, sent_ref.shape[1] - width), 1)
            tail = jnp.where(
                lane == 0,
                high_part,
                jnp.where(lane == 1, mid_part, jnp.where(lane == 2, low_part, 0.0)),
            )
            sent_ref[:, :width] = (middle * out_gain_ref[...]).astype(jnp.bfloat16)
            sent_ref[:, width:] = tail.astype(jnp.bfloat16)


def up_kernel(place_ref, x_ref, w0_ref, w1_ref, w2_ref, w3_ref, out_ref):
    copies, height, units = out_ref.shape
    bands, rows, wide = x_ref.shape
    width = w0_ref.shape[3]
    total = jnp.zeros((rows, units), jnp.float32)
    for k, w_ref in enumerate((w0_ref, w1_ref, w2_ref, w3_ref)):
        features = x_ref[lax.rem(place_ref[0] + bands - k, bands)][:, :width]
        weights = w_ref[:, 0].reshape(units, width)
        total += lax.dot_general(
            features, weights, (((1,), (1,)), ((), ())), preferred_element_type=jnp.float32
        )
    squares = jnp.zeros((rows, 1), jnp.float32)
    for band in range(bands):
        squares += jnp.sum(x_ref[band][:, width:].astype(jnp.float32), axis=1, keepdims=True)
    line = jnp.broadcast_to(to_lanes(squares, units), (height - rows, units))
    for copy in range(copies):
        out_ref[copy, :rows] = total
        out_ref[copy, rows:] = line


def down_kernel(place_ref, sums_ref, w0_ref, w1_ref, w2_ref, w3_ref, out_ref):
    bands, rows, width = out_ref.shape
    total = jnp.sum(sums_ref[...], axis=0)
    factor = lax.rsqrt(to_rows(total[rows : rows + 1], rows) / D + norm_eps)
    upper = jnp.maximum(total[:rows] * factor, 0.0)
    active = (upper * upper).astype(jnp.bfloat16)
    for k, w_ref in enumerate((w0_ref, w1_ref, w2_ref, w3_ref)):
        weights = w_ref[:, 1].reshape(active.shape[1], width)
        out_ref[lax.rem(place_ref[0] + bands - k, bands)] = jnp.dot(
            active, weights, preferred_element_type=jnp.float32
        ).astype(jnp.bfloat16)


VMEM = pl.BlockSpec(memory_space=pltpu.VMEM)
SMEM = pl.BlockSpec(memory_space=pltpu.SMEM)


def whole(shape):
    return pl.BlockSpec(shape, lambda i: (0,) * len(shape))


def attend(role, lengths, hidden, squares, gain, flip_gain, flip, out_gain, kv):
    rows, width = hidden.shape
    count = kv.shape[0]
    groups = width // HEAD
    pairs = 2
    block = (2 * pairs,) + kv.shape[1:]
    return pl.pallas_call(
        functools.partial(attend_kernel, pairs),
        grid=(count // (2 * pairs),),
        out_shape=(
            jax.ShapeDtypeStruct((rows, width), jnp.float32),
            jax.ShapeDtypeStruct((rows, 640), jnp.bfloat16),
        ),
        in_specs=[
            SMEM,
            SMEM,
            whole(hidden.shape),
            whole(squares.shape),
            whole(gain.shape),
            whole(flip_gain.shape),
            whole(flip.shape),
            whole(out_gain.shape),
            pl.BlockSpec(block, lambda i: (i, 0, 0)),
        ],
        out_specs=(whole((rows, width)), whole((rows, 640))),
        scratch_shapes=[
            pltpu.VMEM((groups, rows, HEAD), jnp.float32),
            pltpu.VMEM((groups, rows, HEAD), jnp.float32),
            pltpu.VMEM((rows, HEAD), jnp.float32),
        ],
        compiler_params=pltpu.CompilerParams(vmem_limit_bytes=24 * 1024 * 1024),
    )(role, lengths, hidden, squares, gain, flip_gain, flip, out_gain, kv)


def body(grad_parts, master, moment1, moment2, kv_cache, hidden_in, attn_gain, ffn_gain, lengths):
    role_index = lax.axis_index("role")
    place = lax.axis_index("dp")
    shards = lax.axis_size("dp")
    tensor = lax.axis_size("tensor")
    bands = tensor // BAND
    bf16 = jnp.bfloat16
    band_groups = [[b * BAND + m for m in range(BAND)] for b in range(bands)]
    member_groups = [[b * BAND + m for b in range(bands)] for m in range(BAND)]
    quarter = master.shape[3]

    def learner_pairs(by):
        return [(i, (i + by) % shards) for i in range(shards)]

    grads = grad_parts[0, 0]

    def grad_quarter(owner):
        return lax.dynamic_slice_in_dim(grads, owner * quarter, quarter, 2)

    arriving = [
        lax.ppermute(grad_quarter((place + k) % shards), ("role", "dp"), learner_pairs(k))
        for k in range(1, shards)
    ]

    row_count, steps, width = hidden_in.shape
    rows = row_count * steps
    hidden = hidden_in.astype(jnp.float32).reshape(rows, width)
    squares = pl.pallas_call(
        squares_kernel,
        out_shape=jax.ShapeDtypeStruct((tensor, 8, 128), jnp.float32),
        in_specs=[VMEM],
        out_specs=VMEM,
    )(hidden)
    squares = lax.all_to_all(squares, "tensor", 0, 0, tiled=True)

    feature_start = lax.axis_index("tensor") * width
    gain_attn = lax.dynamic_slice_in_dim(attn_gain, feature_start, width)[None]
    gain_ffn = lax.dynamic_slice_in_dim(ffn_gain, feature_start, width)[None]
    middle, outgoing = attend(
        role_index.astype(jnp.int32)[None],
        lengths,
        hidden,
        squares,
        gain_attn,
        jnp.flip(gain_attn[:, :HEAD], axis=1),
        jnp.flip(hidden[:, :HEAD], axis=1),
        gain_ffn,
        kv_cache[0, :, 0],
    )
    features = lax.ppermute(outgoing, "role", [(1, 0)])
    middle_home = lax.ppermute(middle, "role", [(1, 0)])

    grad_sum = grad_quarter(place).astype(jnp.float32)
    for part in arriving:
        grad_sum = grad_sum + part.astype(jnp.float32)
    new_master = adam_update(grad_sum, master[0], moment1[0], moment2[0])
    synced = new_master.astype(bf16)
    copied = lax.ppermute(synced, "role", [(0, 1)])
    weights_after = jnp.where(role_index == 0, new_master, copied.astype(jnp.float32))[None]

    units = synced.shape[0]
    blocks = synced.reshape(units, 2, BAND, width).transpose(2, 1, 0, 3)
    own = lax.all_to_all(blocks, "tensor", 0, 0, tiled=True, axis_index_groups=band_groups)
    slabs = [own] + [
        lax.ppermute(own, ("role", "dp"), learner_pairs(k)) for k in range(1, shards)
    ]
    gathered = lax.all_to_all(
        jnp.broadcast_to(features[None], (bands,) + features.shape),
        "tensor",
        0,
        0,
        tiled=True,
        axis_index_groups=member_groups,
    )
    place_operand = place.astype(jnp.int32)[None]
    sums = pl.pallas_call(
        up_kernel,
        out_shape=jax.ShapeDtypeStruct((BAND, rows + 8, BAND * units), jnp.float32),
        in_specs=[SMEM] + [VMEM] * 5,
        out_specs=VMEM,
    )(place_operand, gathered, *slabs)
    sums = lax.all_to_all(sums, "tensor", 0, 0, tiled=True, axis_index_groups=band_groups)
    parts = pl.pallas_call(
        down_kernel,
        out_shape=jax.ShapeDtypeStruct((bands, rows, width), bf16),
        in_specs=[SMEM] + [VMEM] * 5,
        out_specs=VMEM,
    )(place_operand, sums, *slabs)
    parts = lax.all_to_all(parts, "tensor", 0, 0, tiled=True, axis_index_groups=member_groups)
    decoded = (middle_home + jnp.sum(parts.astype(jnp.float32), axis=0)).astype(bf16)
    decoded = decoded.reshape(row_count, steps, width)
    returned = lax.ppermute(decoded, "role", [(0, 1)])
    decoded = jnp.where(role_index == 0, decoded, returned)
    return (weights_after, decoded)


def solution(mesh):
    in_specs = (
        P("role", "dp", "tensor", None, None),
        P("role", "tensor", None, "dp"),
        P("role", "tensor", None, "dp"),
        P("role", "tensor", None, "dp"),
        P("role", "dp", "tensor", None, None),
        P("dp", None, "tensor"),
        P(),
        P(),
        P("dp"),
    )
    out_specs = (P("role", "tensor", None, "dp"), P("dp", None, "tensor"))
    return jax.shard_map(body, mesh=mesh, in_specs=in_specs, out_specs=out_specs, check_vma=False)
```

```python
import functools
import math

import jax
import jax.numpy as jnp
from jax import lax
from jax.experimental import pallas as pl
from jax.experimental.pallas import tpu as pltpu
from jax.sharding import PartitionSpec as P

D = 18432
HEAD = 192
STEPS = 4
BAND = 8


beta_one = 0.9
beta_two = 0.95
rate_factor = 0.5
decay_rate = 0.1
adam_eps = 1e-08
norm_eps = 1e-05
step_count = 10


def adam_update(grad_sum, weights, first, second):
    learn_rate = rate_factor / math.sqrt(D)
    first_new = beta_one * first + (1.0 - beta_one) * grad_sum
    second_new = beta_two * second + (1.0 - beta_two) * grad_sum * grad_sum
    corr_one = 1.0 - beta_one**step_count
    corr_two = 1.0 - beta_two**step_count
    ratio = first_new / corr_one / (jnp.sqrt(second_new / corr_two) + adam_eps)
    return weights - learn_rate * (ratio + decay_rate * weights)


def to_lanes(column, lanes):
    rows = column.shape[0]
    here = lax.broadcasted_iota(jnp.int32, (rows, lanes), 0)
    lane = lax.broadcasted_iota(jnp.int32, (rows, lanes), 1)
    return jnp.sum(jnp.where(here == lane, column, 0.0), axis=0, keepdims=True)


def to_rows(line, rows):
    lanes = line.shape[1]
    here = lax.broadcasted_iota(jnp.int32, (rows, lanes), 0)
    lane = lax.broadcasted_iota(jnp.int32, (rows, lanes), 1)
    return jnp.sum(jnp.where(here == lane, line, 0.0), axis=1, keepdims=True)


def three_terms(values):
    high = values.astype(jnp.bfloat16).astype(jnp.float32)
    middle = (values - high).astype(jnp.bfloat16).astype(jnp.float32)
    return high, middle, values - high - middle


def squares_kernel(hidden_ref, out_ref):
    hidden = hidden_ref[...]
    line = to_lanes(jnp.sum(hidden * hidden, axis=1, keepdims=True), 128)
    out_ref[...] = jnp.broadcast_to(line[None], out_ref.shape)


def attend_kernel(
    pairs,
    role_ref,
    len_ref,
    hidden_ref,
    squares_ref,
    gain_ref,
    out_gain_ref,
    kv_ref,
    middle_ref,
    sent_ref,
    normed_ref,
    hidden_parts_ref,
    flip_normed_ref,
):
    step = pl.program_id(0)
    groups = normed_ref.shape[0]
    rows = hidden_ref.shape[0]
    scale = 1.0 / math.sqrt(HEAD)

    @pl.when(role_ref[0] == 1)
    def _():
        @pl.when(step == 0)
        def _():
            total = jnp.sum(squares_ref[...], axis=0)[0:1]
            factor = lax.rsqrt(to_rows(total, rows) / D + norm_eps)
            hidden = hidden_ref[...]
            normed = hidden * factor * gain_ref[...]
            for q in range(groups):
                part = slice(q * HEAD, (q + 1) * HEAD)
                normed_ref[q] = normed[:, part]
                hidden_parts_ref[q] = hidden[:, part]
            across = lax.broadcasted_iota(jnp.int32, (HEAD, HEAD), 0)
            down = lax.broadcasted_iota(jnp.int32, (HEAD, HEAD), 1)
            reverse = jnp.where(across + down == HEAD - 1, 1.0, 0.0).astype(jnp.bfloat16)
            flip_normed_ref[...] = jnp.dot(
                normed_ref[0].astype(jnp.bfloat16), reverse, preferred_element_type=jnp.float32
            )

        high = lax.broadcasted_iota(jnp.int32, (groups * 8, 1), 0) % 8 >= 4
        row_id = lax.broadcasted_iota(jnp.int32, (groups * 8, 8), 0) % 8
        col_id = lax.broadcasted_iota(jnp.int32, (groups * 8, 8), 1)
        fresh_ok = (row_id // 4 == col_id // 4) & (col_id % 4 <= row_id % 4)
        context = kv_ref.shape[1]
        position = lax.broadcasted_iota(jnp.int32, (groups * 8, context), 1)
        for p in range(pairs):
            pair = step * pairs + p
            first = pl.multiple_of(pair * 8, 8)
            query = jnp.concatenate(
                [normed_ref[q, pl.ds(first, 8), :] for q in range(groups)], axis=0
            ).astype(jnp.bfloat16)
            new_keys = flip_normed_ref[pl.ds(first, 8), :].astype(jnp.bfloat16)
            new_values = normed_ref[1, pl.ds(first, 8), :].astype(jnp.bfloat16)
            contract = (((1,), (1,)), ((), ()))
            scores = []
            for half in range(2):
                keys = kv_ref[2 * p + half, :, :HEAD]
                scores.append(
                    lax.dot_general(query, keys, contract, preferred_element_type=jnp.float32)
                )
            cache = jnp.where(high, scores[1], scores[0]) * scale
            length = jnp.where(high, len_ref[2 * pair + 1], len_ref[2 * pair])
            cache = jnp.where(position < length, cache, -jnp.inf)
            fresh = (
                lax.dot_general(query, new_keys, contract, preferred_element_type=jnp.float32)
                * scale
            )
            fresh = jnp.where(fresh_ok, fresh, -jnp.inf)
            top = jnp.maximum(
                jnp.max(cache, axis=1, keepdims=True), jnp.max(fresh, axis=1, keepdims=True)
            )
            cache = jnp.exp(cache - top)
            fresh = jnp.exp(fresh - top)
            total = jnp.sum(cache, axis=1, keepdims=True) + jnp.sum(fresh, axis=1, keepdims=True)
            cache = (cache / total).astype(jnp.bfloat16)
            fresh = (fresh / total).astype(jnp.bfloat16)
            weighed = []
            for half in range(2):
                values = kv_ref[2 * p + half, :, HEAD:]
                weighed.append(jnp.dot(cache, values, preferred_element_type=jnp.float32))
            attended = jnp.where(high, weighed[1], weighed[0]) + jnp.dot(
                fresh, new_values, preferred_element_type=jnp.float32
            )
            for q in range(groups):
                middle_ref[pl.ds(first, 8), q * HEAD : (q + 1) * HEAD] = (
                    hidden_parts_ref[q, pl.ds(first, 8), :] + attended[q * 8 : (q + 1) * 8]
                )

        @pl.when(step == pl.num_programs(0) - 1)
        def _():
            middle = middle_ref[...]
            width = middle.shape[1]
            squares = jnp.sum(middle * middle, axis=1, keepdims=True)
            lane = lax.broadcasted_iota(jnp.int32, (rows, sent_ref.shape[1] - width), 1)
            tail = jnp.zeros(lane.shape, jnp.float32)
            for i, term in enumerate(three_terms(squares)):
                tail = jnp.where(lane == i, term, tail)
            sent_ref[:, :width] = (middle * out_gain_ref[...]).astype(jnp.bfloat16)
            sent_ref[:, width:] = tail.astype(jnp.bfloat16)


def adam_kernel(place_ref, grad_ref, g1_ref, g2_ref, g3_ref, w_ref, m1_ref, m2_ref, new_ref, blocks_ref):
    members, halves, units, width = blocks_ref.shape
    step = 2 * width
    for half in range(halves):
        for i in range(members // 2):
            cut = slice(i * step, (i + 1) * step)
            grad_sum = grad_ref[:, half, cut].astype(jnp.float32)
            for ref in (g1_ref, g2_ref, g3_ref):
                grad_sum = grad_sum + ref[:, half, cut].astype(jnp.float32)
            new = adam_update(
                grad_sum, w_ref[:, half, cut], m1_ref[:, half, cut], m2_ref[:, half, cut]
            )
            new_ref[:, half, cut] = new
            blocks_ref[2 * i, half] = new[:, :width].astype(jnp.bfloat16)
            blocks_ref[2 * i + 1, half] = new[:, width:].astype(jnp.bfloat16)


def up_kernel(place_ref, x0_ref, x1_ref, x2_ref, x3_ref, w0_ref, w1_ref, w2_ref, w3_ref, out_ref):
    copies, height, units = out_ref.shape
    bands = 4
    rows = x0_ref.shape[0]
    width = w0_ref.shape[3]
    x_refs = (x0_ref, x1_ref, x2_ref, x3_ref)
    w_refs = (w0_ref, w1_ref, w2_ref, w3_ref)
    shift = lax.rem(place_ref[1] - place_ref[0] + bands, bands)
    for value in range(bands):

        @pl.when(shift == value)
        def _(value=value):
            total = jnp.zeros((rows, units), jnp.float32)
            squares = jnp.zeros((rows, 1), jnp.float32)
            for k in range(bands):
                x_ref = x_refs[(k + value) % bands]
                total += lax.dot_general(
                    x_ref[:, :width],
                    w_refs[k][:, 0].reshape(units, width),
                    (((1,), (1,)), ((), ())),
                    preferred_element_type=jnp.float32,
                )
                squares += jnp.sum(x_ref[:, width:].astype(jnp.float32), axis=1, keepdims=True)
            line = to_lanes(squares, units)
            row = lax.broadcasted_iota(jnp.int32, (height - rows, units), 0)
            tail = jnp.zeros((height - rows, units), jnp.float32)
            for i, term in enumerate(three_terms(line)):
                tail = jnp.where(row == i, term, tail)
            total = total.astype(out_ref.dtype)
            tail = tail.astype(out_ref.dtype)
            for copy in range(copies):
                out_ref[copy, :rows] = total
                out_ref[copy, rows:] = tail


def down_kernel(place_ref, sums_ref, w0_ref, w1_ref, w2_ref, w3_ref, out_ref):
    roles, bands, rows, width = out_ref.shape
    total = jnp.sum(sums_ref[...].astype(jnp.float32), axis=0)
    squares = jnp.sum(total[rows : rows + 8], axis=0, keepdims=True)
    factor = lax.rsqrt(to_rows(squares, rows) / D + norm_eps)
    upper = jnp.maximum(total[:rows] * factor, 0.0)
    active = (upper * upper).astype(jnp.bfloat16)
    for k, w_ref in enumerate((w0_ref, w1_ref, w2_ref, w3_ref)):
        weights = w_ref[:, 1].reshape(active.shape[1], width)
        band = lax.rem(place_ref[0] + bands - k, bands)
        part = jnp.dot(active, weights, preferred_element_type=jnp.float32).astype(jnp.bfloat16)
        for role in range(roles):
            out_ref[role, band] = part


VMEM = pl.BlockSpec(memory_space=pltpu.VMEM)
SMEM = pl.BlockSpec(memory_space=pltpu.SMEM)


def whole(shape):
    return pl.BlockSpec(shape, lambda i: (0,) * len(shape))


def attend(role, lengths, hidden, squares, gain, out_gain, kv):
    rows, width = hidden.shape
    count = kv.shape[0]
    groups = width // HEAD
    pairs = 2
    block = (2 * pairs,) + kv.shape[1:]
    return pl.pallas_call(
        functools.partial(attend_kernel, pairs),
        grid=(count // (2 * pairs),),
        out_shape=(
            jax.ShapeDtypeStruct((rows, width), jnp.float32),
            jax.ShapeDtypeStruct((rows, 640), jnp.bfloat16),
        ),
        in_specs=[
            SMEM,
            SMEM,
            whole(hidden.shape),
            whole(squares.shape),
            whole(gain.shape),
            whole(out_gain.shape),
            pl.BlockSpec(block, lambda i: (i, 0, 0)),
        ],
        out_specs=(whole((rows, width)), whole((rows, 640))),
        scratch_shapes=[
            pltpu.VMEM((groups, rows, HEAD), jnp.float32),
            pltpu.VMEM((groups, rows, HEAD), jnp.float32),
            pltpu.VMEM((rows, HEAD), jnp.float32),
        ],
        compiler_params=pltpu.CompilerParams(vmem_limit_bytes=24 * 1024 * 1024),
    )(role, lengths, hidden, squares, gain, out_gain, kv)


def body(grad_parts, master, moment1, moment2, kv_cache, hidden_in, attn_gain, ffn_gain, lengths):
    role_index = lax.axis_index("role")
    place = lax.axis_index("dp")
    shards = lax.axis_size("dp")
    tensor = lax.axis_size("tensor")
    bands = tensor // BAND
    bf16 = jnp.bfloat16
    band_groups = [[b * BAND + m for m in range(BAND)] for b in range(bands)]
    member_groups = [[b * BAND + m for b in range(bands)] for m in range(BAND)]
    quarter = master.shape[3]

    def learner_pairs(by):
        return [(i, (i + by) % shards) for i in range(shards)]

    grads = grad_parts[0, 0]

    def grad_quarter(owner):
        return lax.dynamic_slice_in_dim(grads, owner * quarter, quarter, 2)

    arriving = [
        lax.ppermute(grad_quarter((place + k) % shards), ("role", "dp"), learner_pairs(k))
        for k in range(1, shards)
    ]

    row_count, steps, width = hidden_in.shape
    rows = row_count * steps
    hidden = hidden_in.astype(jnp.float32).reshape(rows, width)
    squares = pl.pallas_call(
        squares_kernel,
        out_shape=jax.ShapeDtypeStruct((tensor, 8, 128), jnp.float32),
        in_specs=[VMEM],
        out_specs=VMEM,
    )(hidden)
    squares = lax.all_to_all(squares, "tensor", 0, 0, tiled=True)

    feature_start = lax.axis_index("tensor") * width
    gain_attn = lax.dynamic_slice_in_dim(attn_gain, feature_start, width)[None]
    gain_ffn = lax.dynamic_slice_in_dim(ffn_gain, feature_start, width)[None]
    middle, outgoing = attend(
        role_index.astype(jnp.int32)[None],
        lengths,
        hidden,
        squares,
        gain_attn,
        gain_ffn,
        kv_cache[0, :, 0],
    )

    def to_holders(by):
        pairs = []
        for d in range(shards):
            for b in range(bands):
                for m in range(BAND):
                    source = (shards + d) * tensor + b * BAND + m
                    pairs.append((source, d * tensor + (b + by) % bands * BAND + m))
        return pairs

    features = [
        lax.ppermute(outgoing, ("role", "dp", "tensor"), to_holders(k)) for k in range(bands)
    ]
    middle_home = lax.ppermute(middle, "role", [(1, 0)])
    middle = jnp.where(role_index == 0, middle_home, middle)

    place_operand = jnp.stack([place, lax.axis_index("tensor") // BAND]).astype(jnp.int32)
    units = master.shape[1]
    arriving, outgoing = lax.optimization_barrier((arriving, outgoing))
    flat = pl.BlockSpec((units, 2, quarter), lambda i, place_ref: (0, 0, 0))
    new_master, blocks = pl.pallas_call(
        adam_kernel,
        out_shape=(
            jax.ShapeDtypeStruct((units, 2, quarter), jnp.float32),
            jax.ShapeDtypeStruct((BAND, 2, units, width), bf16),
        ),
        grid_spec=pltpu.PrefetchScalarGridSpec(
            num_scalar_prefetch=1,
            grid=(1,),
            in_specs=[pl.BlockSpec((units, 2, quarter), lambda i, place_ref: (0, 0, place_ref[0]))]
            + [flat] * 6,
            out_specs=(
                flat,
                pl.BlockSpec((BAND, 2, units, width), lambda i, place_ref: (0, 0, 0, 0)),
            ),
        ),
        compiler_params=pltpu.CompilerParams(vmem_limit_bytes=24 * 1024 * 1024),
    )(place_operand, grads, *arriving, master[0], moment1[0], moment2[0])
    copied = lax.ppermute(new_master, "role", [(0, 1)]).astype(bf16).astype(jnp.float32)
    weights_after = jnp.where(role_index == 0, new_master, copied)[None]

    own = lax.all_to_all(blocks, "tensor", 0, 0, tiled=True, axis_index_groups=band_groups)
    slabs = [own] + [
        lax.ppermute(own, ("role", "dp"), learner_pairs(k)) for k in range(1, shards)
    ]
    sums = pl.pallas_call(
        up_kernel,
        out_shape=jax.ShapeDtypeStruct((BAND, rows + 16, BAND * units), bf16),
        in_specs=[SMEM] + [VMEM] * 8,
        out_specs=VMEM,
    )(place_operand, *features, *slabs)
    sums = lax.all_to_all(sums, "tensor", 0, 0, tiled=True, axis_index_groups=band_groups)
    parts = pl.pallas_call(
        down_kernel,
        out_shape=jax.ShapeDtypeStruct((2, bands, rows, width), bf16),
        in_specs=[SMEM] + [VMEM] * 5,
        out_specs=VMEM,
    )(place_operand, sums, *slabs)
    parts = parts.reshape(2 * bands, rows, width)
    home_groups = [
        [r * tensor + b * BAND + m for r in range(2) for b in range(bands)] for m in range(BAND)
    ]
    parts = lax.all_to_all(
        parts, ("role", "tensor"), 0, 0, tiled=True, axis_index_groups=home_groups
    )
    decoded = (middle + jnp.sum(parts[:bands].astype(jnp.float32), axis=0)).astype(bf16)
    return (weights_after, decoded.reshape(row_count, steps, width))


def solution(mesh):
    in_specs = (
        P("role", "dp", "tensor", None, None),
        P("role", "tensor", None, "dp"),
        P("role", "tensor", None, "dp"),
        P("role", "tensor", None, "dp"),
        P("role", "dp", "tensor", None, None),
        P("dp", None, "tensor"),
        P(),
        P(),
        P("dp"),
    )
    out_specs = (P("role", "tensor", None, "dp"), P("dp", None, "tensor"))
    return jax.shard_map(body, mesh=mesh, in_specs=in_specs, out_specs=out_specs, check_vma=False)
```

```python
import functools
import math

import jax
import jax.numpy as jnp
from jax import lax
from jax.experimental import pallas as pl
from jax.experimental.pallas import tpu as pltpu
from jax.sharding import PartitionSpec as P

D = 18432
HEAD = 192
STEPS = 4
BAND = 8


beta_one = 0.9
beta_two = 0.95
rate_factor = 0.5
decay_rate = 0.1
adam_eps = 1e-08
norm_eps = 1e-05
step_count = 10


def adam_update(grad_sum, weights, first, second):
    learn_rate = rate_factor / math.sqrt(D)
    first_new = beta_one * first + (1.0 - beta_one) * grad_sum
    second_new = beta_two * second + (1.0 - beta_two) * grad_sum * grad_sum
    corr_one = 1.0 - beta_one**step_count
    corr_two = 1.0 - beta_two**step_count
    ratio = first_new / corr_one / (jnp.sqrt(second_new / corr_two) + adam_eps)
    return weights - learn_rate * (ratio + decay_rate * weights)


def to_lanes(column, lanes):
    rows = column.shape[0]
    here = lax.broadcasted_iota(jnp.int32, (rows, lanes), 0)
    lane = lax.broadcasted_iota(jnp.int32, (rows, lanes), 1)
    return jnp.sum(jnp.where(here == lane, column, 0.0), axis=0, keepdims=True)


def to_rows(line, rows):
    lanes = line.shape[1]
    here = lax.broadcasted_iota(jnp.int32, (rows, lanes), 0)
    lane = lax.broadcasted_iota(jnp.int32, (rows, lanes), 1)
    return jnp.sum(jnp.where(here == lane, line, 0.0), axis=1, keepdims=True)


def three_terms(values):
    high = values.astype(jnp.bfloat16).astype(jnp.float32)
    middle = (values - high).astype(jnp.bfloat16).astype(jnp.float32)
    return high, middle, values - high - middle


def squares_kernel(hidden_ref, out_ref):
    hidden = hidden_ref[...]
    line = to_lanes(jnp.sum(hidden * hidden, axis=1, keepdims=True), 128)
    out_ref[...] = jnp.broadcast_to(line[None], out_ref.shape)


def attend_kernel(
    pairs,
    len_ref,
    hidden_ref,
    squares_ref,
    gain_ref,
    out_gain_ref,
    kv_ref,
    middle_ref,
    sent_ref,
    normed_ref,
    hidden_parts_ref,
    flip_normed_ref,
):
    step = pl.program_id(0)
    groups = normed_ref.shape[0]
    rows = hidden_ref.shape[0]
    scale = 1.0 / math.sqrt(HEAD)

    @pl.when(step == 0)
    def _():
        total = jnp.sum(squares_ref[...], axis=0)[0:1]
        factor = lax.rsqrt(to_rows(total, rows) / D + norm_eps)
        hidden = hidden_ref[...]
        normed = hidden * factor * gain_ref[...]
        for q in range(groups):
            part = slice(q * HEAD, (q + 1) * HEAD)
            normed_ref[q] = normed[:, part]
            hidden_parts_ref[q] = hidden[:, part]
        across = lax.broadcasted_iota(jnp.int32, (HEAD, HEAD), 0)
        down = lax.broadcasted_iota(jnp.int32, (HEAD, HEAD), 1)
        reverse = jnp.where(across + down == HEAD - 1, 1.0, 0.0).astype(jnp.bfloat16)
        flip_normed_ref[...] = jnp.dot(
            normed_ref[0].astype(jnp.bfloat16), reverse, preferred_element_type=jnp.float32
        )

    high = lax.broadcasted_iota(jnp.int32, (groups * 8, 1), 0) % 8 >= 4
    row_id = lax.broadcasted_iota(jnp.int32, (groups * 8, 8), 0) % 8
    col_id = lax.broadcasted_iota(jnp.int32, (groups * 8, 8), 1)
    fresh_ok = (row_id // 4 == col_id // 4) & (col_id % 4 <= row_id % 4)
    context = kv_ref.shape[1]
    position = lax.broadcasted_iota(jnp.int32, (groups * 8, context), 1)
    for p in range(pairs):
        pair = step * pairs + p
        first = pl.multiple_of(pair * 8, 8)
        query = jnp.concatenate(
            [normed_ref[q, pl.ds(first, 8), :] for q in range(groups)], axis=0
        ).astype(jnp.bfloat16)
        new_keys = flip_normed_ref[pl.ds(first, 8), :].astype(jnp.bfloat16)
        new_values = normed_ref[1, pl.ds(first, 8), :].astype(jnp.bfloat16)
        contract = (((1,), (1,)), ((), ()))
        scores = []
        for half in range(2):
            keys = kv_ref[2 * p + half, :, :HEAD]
            scores.append(
                lax.dot_general(query, keys, contract, preferred_element_type=jnp.float32)
            )
        cache = jnp.where(high, scores[1], scores[0]) * scale
        length = jnp.where(high, len_ref[2 * pair + 1], len_ref[2 * pair])
        cache = jnp.where(position < length, cache, -jnp.inf)
        fresh = (
            lax.dot_general(query, new_keys, contract, preferred_element_type=jnp.float32)
            * scale
        )
        fresh = jnp.where(fresh_ok, fresh, -jnp.inf)
        top = jnp.maximum(
            jnp.max(cache, axis=1, keepdims=True), jnp.max(fresh, axis=1, keepdims=True)
        )
        cache = jnp.exp(cache - top)
        fresh = jnp.exp(fresh - top)
        total = jnp.sum(cache, axis=1, keepdims=True) + jnp.sum(fresh, axis=1, keepdims=True)
        cache = (cache / total).astype(jnp.bfloat16)
        fresh = (fresh / total).astype(jnp.bfloat16)
        weighed = []
        for half in range(2):
            values = kv_ref[2 * p + half, :, HEAD:]
            weighed.append(jnp.dot(cache, values, preferred_element_type=jnp.float32))
        attended = jnp.where(high, weighed[1], weighed[0]) + jnp.dot(
            fresh, new_values, preferred_element_type=jnp.float32
        )
        for q in range(groups):
            middle_ref[pl.ds(first, 8), q * HEAD : (q + 1) * HEAD] = (
                hidden_parts_ref[q, pl.ds(first, 8), :] + attended[q * 8 : (q + 1) * 8]
            )

    @pl.when(step == pl.num_programs(0) - 1)
    def _():
        middle = middle_ref[...]
        width = middle.shape[1]
        squares = jnp.sum(middle * middle, axis=1, keepdims=True)
        lane = lax.broadcasted_iota(jnp.int32, (rows, sent_ref.shape[1] - width), 1)
        tail = jnp.zeros(lane.shape, jnp.float32)
        for i, term in enumerate(three_terms(squares)):
            tail = jnp.where(lane == i, term, tail)
        sent_ref[:, :width] = (middle * out_gain_ref[...]).astype(jnp.bfloat16)
        sent_ref[:, width:] = tail.astype(jnp.bfloat16)


def adam_kernel(place_ref, grad_ref, g1_ref, g2_ref, g3_ref, w_ref, m1_ref, m2_ref, new_ref, blocks_ref):
    members, halves, units, width = blocks_ref.shape
    step = 2 * width
    for half in range(halves):
        for i in range(members // 2):
            cut = slice(i * step, (i + 1) * step)
            grad_sum = grad_ref[:, half, cut].astype(jnp.float32)
            for ref in (g1_ref, g2_ref, g3_ref):
                grad_sum = grad_sum + ref[:, half, cut].astype(jnp.float32)
            new = adam_update(
                grad_sum, w_ref[:, half, cut], m1_ref[:, half, cut], m2_ref[:, half, cut]
            )
            new_ref[:, half, cut] = new
            blocks_ref[2 * i, half] = new[:, :width].astype(jnp.bfloat16)
            blocks_ref[2 * i + 1, half] = new[:, width:].astype(jnp.bfloat16)


def up_kernel(place_ref, x_ref, w0_ref, w1_ref, w2_ref, w3_ref, out_ref):
    copies, height, units = out_ref.shape
    bands, rows, _ = x_ref.shape
    width = w0_ref.shape[3]
    total = jnp.zeros((rows, units), jnp.float32)
    squares = jnp.zeros((rows, 1), jnp.float32)
    for k, w_ref in enumerate((w0_ref, w1_ref, w2_ref, w3_ref)):
        x = x_ref[lax.rem(place_ref[0] + bands - k, bands)]
        total += lax.dot_general(
            x[:, :width],
            w_ref[:, 0].reshape(units, width),
            (((1,), (1,)), ((), ())),
            preferred_element_type=jnp.float32,
        )
        squares += jnp.sum(x[:, width:].astype(jnp.float32), axis=1, keepdims=True)
    line = to_lanes(squares, units)
    row = lax.broadcasted_iota(jnp.int32, (height - rows, units), 0)
    tail = jnp.zeros((height - rows, units), jnp.float32)
    for i, term in enumerate(three_terms(line)):
        tail = jnp.where(row == i, term, tail)
    total = total.astype(out_ref.dtype)
    tail = tail.astype(out_ref.dtype)
    for copy in range(copies):
        out_ref[copy, :rows] = total
        out_ref[copy, rows:] = tail


def down_kernel(place_ref, sums_ref, w0_ref, w1_ref, w2_ref, w3_ref, out_ref):
    roles, bands, rows, width = out_ref.shape
    total = jnp.sum(sums_ref[...].astype(jnp.float32), axis=0)
    squares = jnp.sum(total[rows : rows + 8], axis=0, keepdims=True)
    factor = lax.rsqrt(to_rows(squares, rows) / D + norm_eps)
    upper = jnp.maximum(total[:rows] * factor, 0.0)
    active = (upper * upper).astype(jnp.bfloat16)
    for k, w_ref in enumerate((w0_ref, w1_ref, w2_ref, w3_ref)):
        weights = w_ref[:, 1].reshape(active.shape[1], width)
        band = lax.rem(place_ref[0] + bands - k, bands)
        part = jnp.dot(active, weights, preferred_element_type=jnp.float32).astype(jnp.bfloat16)
        for role in range(roles):
            out_ref[role, band] = part


VMEM = pl.BlockSpec(memory_space=pltpu.VMEM)
SMEM = pl.BlockSpec(memory_space=pltpu.SMEM)


def whole(shape):
    return pl.BlockSpec(shape, lambda i: (0,) * len(shape))


def attend(lengths, hidden, squares, gain, out_gain, kv):
    rows, width = hidden.shape
    count = kv.shape[0]
    groups = width // HEAD
    pairs = 2
    block = (2 * pairs,) + kv.shape[1:]
    return pl.pallas_call(
        functools.partial(attend_kernel, pairs),
        grid=(count // (2 * pairs),),
        out_shape=(
            jax.ShapeDtypeStruct((rows, width), jnp.float32),
            jax.ShapeDtypeStruct((rows, 640), jnp.bfloat16),
        ),
        in_specs=[
            SMEM,
            whole(hidden.shape),
            whole(squares.shape),
            whole(gain.shape),
            whole(out_gain.shape),
            pl.BlockSpec(block, lambda i: (i, 0, 0)),
        ],
        out_specs=(whole((rows, width)), whole((rows, 640))),
        scratch_shapes=[
            pltpu.VMEM((groups, rows, HEAD), jnp.float32),
            pltpu.VMEM((groups, rows, HEAD), jnp.float32),
            pltpu.VMEM((rows, HEAD), jnp.float32),
        ],
        compiler_params=pltpu.CompilerParams(vmem_limit_bytes=24 * 1024 * 1024),
    )(lengths, hidden, squares, gain, out_gain, kv)


def body(grad_parts, master, moment1, moment2, kv_cache, hidden_in, attn_gain, ffn_gain, lengths):
    role_index = lax.axis_index("role")
    place = lax.axis_index("dp")
    shards = lax.axis_size("dp")
    tensor = lax.axis_size("tensor")
    bands = tensor // BAND
    bf16 = jnp.bfloat16
    band_groups = [[b * BAND + m for m in range(BAND)] for b in range(bands)]
    member_groups = [[b * BAND + m for b in range(bands)] for m in range(BAND)]
    quarter = master.shape[3]

    grads = grad_parts[0, 0]
    row_count, steps, width = hidden_in.shape
    rows = row_count * steps
    units = master.shape[1]
    place_operand = place.astype(jnp.int32)[None]
    wide = 640

    def learner_pairs(by):
        return [(i, (i + by) % shards) for i in range(shards)]

    def grad_quarter(owner):
        return lax.dynamic_slice_in_dim(grads, owner * quarter, quarter, 2)

    def learn():
        arriving = [
            lax.ppermute(grad_quarter((place + k) % shards), ("role", "dp"), learner_pairs(k))
            for k in range(1, shards)
        ]
        flat = pl.BlockSpec((units, 2, quarter), lambda i, place_ref: (0, 0, 0))
        new_master, blocks = pl.pallas_call(
            adam_kernel,
            out_shape=(
                jax.ShapeDtypeStruct((units, 2, quarter), jnp.float32),
                jax.ShapeDtypeStruct((BAND, 2, units, width), bf16),
            ),
            grid_spec=pltpu.PrefetchScalarGridSpec(
                num_scalar_prefetch=1,
                grid=(1,),
                in_specs=[
                    pl.BlockSpec((units, 2, quarter), lambda i, place_ref: (0, 0, place_ref[0]))
                ]
                + [flat] * 6,
                out_specs=(
                    flat,
                    pl.BlockSpec((BAND, 2, units, width), lambda i, place_ref: (0, 0, 0, 0)),
                ),
            ),
            compiler_params=pltpu.CompilerParams(vmem_limit_bytes=24 * 1024 * 1024),
        )(place_operand, grads, *arriving, master[0], moment1[0], moment2[0])
        own = lax.all_to_all(blocks, "tensor", 0, 0, tiled=True, axis_index_groups=band_groups)
        return (
            new_master,
            own,
            jnp.zeros((bands, rows, wide), bf16),
            jnp.zeros((rows, width), jnp.float32),
        )

    def roll_out():
        hidden = hidden_in.astype(jnp.float32).reshape(rows, width)
        squares = pl.pallas_call(
            squares_kernel,
            out_shape=jax.ShapeDtypeStruct((tensor, 8, 128), jnp.float32),
            in_specs=[VMEM],
            out_specs=VMEM,
        )(hidden)
        squares = lax.all_to_all(squares, "tensor", 0, 0, tiled=True)
        feature_start = lax.axis_index("tensor") * width
        middle, outgoing = attend(
            lengths,
            hidden,
            squares,
            lax.dynamic_slice_in_dim(attn_gain, feature_start, width)[None],
            lax.dynamic_slice_in_dim(ffn_gain, feature_start, width)[None],
            kv_cache[0, :, 0],
        )
        features = lax.all_to_all(
            jnp.broadcast_to(outgoing[None], (bands, rows, wide)),
            "tensor",
            0,
            0,
            tiled=True,
            axis_index_groups=member_groups,
        )
        return (
            jnp.zeros((units, 2, quarter), jnp.float32),
            jnp.zeros((BAND, 2, units, width), bf16),
            features,
            middle,
        )

    new_master, own, features, middle = lax.cond(role_index == 0, learn, roll_out)
    features = lax.ppermute(features, "role", [(1, 0)])
    slabs = [own] + [
        lax.ppermute(own, ("role", "dp"), learner_pairs(k)) for k in range(1, shards)
    ]
    middle_home = lax.ppermute(middle, "role", [(1, 0)])
    middle = jnp.where(role_index == 0, middle_home, middle)
    copied = lax.ppermute(new_master, "role", [(0, 1)]).astype(bf16).astype(jnp.float32)
    weights_after = jnp.where(role_index == 0, new_master, copied)[None]

    sums = pl.pallas_call(
        up_kernel,
        out_shape=jax.ShapeDtypeStruct((BAND, rows + 16, BAND * units), bf16),
        in_specs=[SMEM] + [VMEM] * 5,
        out_specs=VMEM,
    )(place_operand, features, *slabs)
    sums = lax.all_to_all(sums, "tensor", 0, 0, tiled=True, axis_index_groups=band_groups)
    parts = pl.pallas_call(
        down_kernel,
        out_shape=jax.ShapeDtypeStruct((2, bands, rows, width), bf16),
        in_specs=[SMEM] + [VMEM] * 5,
        out_specs=VMEM,
    )(place_operand, sums, *slabs)
    parts = parts.reshape(2 * bands, rows, width)
    home_groups = [
        [r * tensor + b * BAND + m for r in range(2) for b in range(bands)] for m in range(BAND)
    ]
    parts = lax.all_to_all(
        parts, ("role", "tensor"), 0, 0, tiled=True, axis_index_groups=home_groups
    )
    decoded = (middle + jnp.sum(parts[:bands].astype(jnp.float32), axis=0)).astype(bf16)
    return (weights_after, decoded.reshape(row_count, steps, width))


def solution(mesh):
    in_specs = (
        P("role", "dp", "tensor", None, None),
        P("role", "tensor", None, "dp"),
        P("role", "tensor", None, "dp"),
        P("role", "tensor", None, "dp"),
        P("role", "dp", "tensor", None, None),
        P("dp", None, "tensor"),
        P(),
        P(),
        P("dp"),
    )
    out_specs = (P("role", "tensor", None, "dp"), P("dp", None, "tensor"))
    return jax.shard_map(body, mesh=mesh, in_specs=in_specs, out_specs=out_specs, check_vma=False)
```

```python
import functools
import math

import jax
import jax.numpy as jnp
from jax import lax
from jax.experimental import pallas as pl
from jax.experimental.pallas import tpu as pltpu
from jax.sharding import PartitionSpec as P

D = 18432
HEAD = 192
STEPS = 4
BAND = 8


beta_one = 0.9
beta_two = 0.95
rate_factor = 0.5
decay_rate = 0.1
adam_eps = 1e-08
norm_eps = 1e-05
step_count = 10


def adam_update(grad_sum, weights, first, second):
    learn_rate = rate_factor / math.sqrt(D)
    first_new = beta_one * first + (1.0 - beta_one) * grad_sum
    second_new = beta_two * second + (1.0 - beta_two) * grad_sum * grad_sum
    corr_one = 1.0 - beta_one**step_count
    corr_two = 1.0 - beta_two**step_count
    ratio = first_new / corr_one / (jnp.sqrt(second_new / corr_two) + adam_eps)
    return weights - learn_rate * (ratio + decay_rate * weights)


def to_lanes(column, lanes):
    rows = column.shape[0]
    here = lax.broadcasted_iota(jnp.int32, (rows, lanes), 0)
    lane = lax.broadcasted_iota(jnp.int32, (rows, lanes), 1)
    return jnp.sum(jnp.where(here == lane, column, 0.0), axis=0, keepdims=True)


def to_rows(line, rows):
    lanes = line.shape[1]
    here = lax.broadcasted_iota(jnp.int32, (rows, lanes), 0)
    lane = lax.broadcasted_iota(jnp.int32, (rows, lanes), 1)
    return jnp.sum(jnp.where(here == lane, line, 0.0), axis=1, keepdims=True)


def three_terms(values):
    high = values.astype(jnp.bfloat16).astype(jnp.float32)
    middle = (values - high).astype(jnp.bfloat16).astype(jnp.float32)
    return high, middle, values - high - middle


def squares_kernel(hidden_ref, out_ref):
    hidden = hidden_ref[...].astype(jnp.float32)
    squares = jnp.sum(hidden * hidden, axis=2, keepdims=True)
    shape = hidden.shape[:2] + (out_ref.shape[2],)
    row = lax.broadcasted_iota(jnp.int32, shape, 0) * shape[1]
    row = row + lax.broadcasted_iota(jnp.int32, shape, 1)
    lane = lax.broadcasted_iota(jnp.int32, shape, 2)
    line = jnp.sum(jnp.where(lane == row, squares, 0.0), axis=(0, 1))
    out_ref[...] = jnp.broadcast_to(line[None, None], out_ref.shape)


def attend_kernel(
    pairs,
    len_ref,
    hidden_ref,
    squares_ref,
    gain_ref,
    out_gain_ref,
    kv_ref,
    sent_ref,
    halves_ref,
    middle_ref,
    normed_ref,
    hidden_parts_ref,
    flip_normed_ref,
):
    step = pl.program_id(0)
    groups = normed_ref.shape[0]
    rows = hidden_ref.shape[0]
    scale = 1.0 / math.sqrt(HEAD)

    @pl.when(step == 0)
    def _():
        total = jnp.sum(squares_ref[...], axis=0)[0:1]
        factor = lax.rsqrt(to_rows(total, rows) / D + norm_eps)
        hidden = hidden_ref[...]
        normed = hidden * factor * gain_ref[...]
        for q in range(groups):
            part = slice(q * HEAD, (q + 1) * HEAD)
            normed_ref[q] = normed[:, part]
            hidden_parts_ref[q] = hidden[:, part]
        across = lax.broadcasted_iota(jnp.int32, (HEAD, HEAD), 0)
        down = lax.broadcasted_iota(jnp.int32, (HEAD, HEAD), 1)
        reverse = jnp.where(across + down == HEAD - 1, 1.0, 0.0).astype(jnp.bfloat16)
        flip_normed_ref[...] = jnp.dot(
            normed_ref[0].astype(jnp.bfloat16), reverse, preferred_element_type=jnp.float32
        )

    high = lax.broadcasted_iota(jnp.int32, (groups * 8, 1), 0) % 8 >= 4
    row_id = lax.broadcasted_iota(jnp.int32, (groups * 8, 8), 0) % 8
    col_id = lax.broadcasted_iota(jnp.int32, (groups * 8, 8), 1)
    fresh_ok = (row_id // 4 == col_id // 4) & (col_id % 4 <= row_id % 4)
    context = kv_ref.shape[1]
    position = lax.broadcasted_iota(jnp.int32, (groups * 8, context), 1)
    for p in range(pairs):
        pair = step * pairs + p
        first = pl.multiple_of(pair * 8, 8)
        query = jnp.concatenate(
            [normed_ref[q, pl.ds(first, 8), :] for q in range(groups)], axis=0
        ).astype(jnp.bfloat16)
        new_keys = flip_normed_ref[pl.ds(first, 8), :].astype(jnp.bfloat16)
        new_values = normed_ref[1, pl.ds(first, 8), :].astype(jnp.bfloat16)
        contract = (((1,), (1,)), ((), ()))
        scores = []
        for half in range(2):
            keys = kv_ref[2 * p + half, :, :HEAD]
            scores.append(
                lax.dot_general(query, keys, contract, preferred_element_type=jnp.float32)
            )
        cache = jnp.where(high, scores[1], scores[0]) * scale
        length = jnp.where(high, len_ref[2 * pair + 1], len_ref[2 * pair])
        cache = jnp.where(position < length, cache, -jnp.inf)
        fresh = (
            lax.dot_general(query, new_keys, contract, preferred_element_type=jnp.float32)
            * scale
        )
        fresh = jnp.where(fresh_ok, fresh, -jnp.inf)
        top = jnp.maximum(
            jnp.max(cache, axis=1, keepdims=True), jnp.max(fresh, axis=1, keepdims=True)
        )
        cache = jnp.exp(cache - top)
        fresh = jnp.exp(fresh - top)
        total = jnp.sum(cache, axis=1, keepdims=True) + jnp.sum(fresh, axis=1, keepdims=True)
        cache = (cache / total).astype(jnp.bfloat16)
        fresh = (fresh / total).astype(jnp.bfloat16)
        weighed = []
        for half in range(2):
            values = kv_ref[2 * p + half, :, HEAD:]
            weighed.append(jnp.dot(cache, values, preferred_element_type=jnp.float32))
        attended = jnp.where(high, weighed[1], weighed[0]) + jnp.dot(
            fresh, new_values, preferred_element_type=jnp.float32
        )
        for q in range(groups):
            middle_ref[pl.ds(first, 8), q * HEAD : (q + 1) * HEAD] = (
                hidden_parts_ref[q, pl.ds(first, 8), :] + attended[q * 8 : (q + 1) * 8]
            )

    @pl.when(step == pl.num_programs(0) - 1)
    def _():
        middle = middle_ref[...]
        width = middle.shape[1]
        squares = jnp.sum(middle * middle, axis=1, keepdims=True)
        lane = lax.broadcasted_iota(jnp.int32, (rows, sent_ref.shape[1] - width), 1)
        tail = jnp.zeros(lane.shape, jnp.float32)
        for i, term in enumerate(three_terms(squares)):
            tail = jnp.where(lane == i, term, tail)
        sent_ref[:, :width] = (middle * out_gain_ref[...]).astype(jnp.bfloat16)
        sent_ref[:, width:] = tail.astype(jnp.bfloat16)
        rounded = middle.astype(jnp.bfloat16)
        halves_ref[0, :, :width] = rounded
        halves_ref[1, :, :width] = (middle - rounded.astype(jnp.float32)).astype(jnp.bfloat16)
        halves_ref[:, :, width:] = jnp.zeros((2,) + lane.shape, jnp.bfloat16)


def split_kernel(grads_ref, out_ref, sems):
    quarter = out_ref.shape[3]
    copies = [
        pltpu.make_async_copy(
            grads_ref.at[:, :, pl.ds(k * quarter, quarter)], out_ref.at[k], sems.at[k]
        )
        for k in range(out_ref.shape[0])
    ]
    for copy in copies:
        copy.start()
    for copy in copies:
        copy.wait()


def adam_kernel(grads_ref, w_ref, m1_ref, m2_ref, new_ref, blocks_ref):
    members, halves, units, width = blocks_ref.shape
    step = 2 * width
    for half in range(halves):
        for i in range(members // 2):
            cut = slice(i * step, (i + 1) * step)
            grad_sum = jnp.sum(grads_ref[:, :, half, cut].astype(jnp.float32), axis=0)
            new = adam_update(
                grad_sum, w_ref[:, half, cut], m1_ref[:, half, cut], m2_ref[:, half, cut]
            )
            new_ref[:, half, cut] = new
            blocks_ref[2 * i, half] = new[:, :width].astype(jnp.bfloat16)
            blocks_ref[2 * i + 1, half] = new[:, width:].astype(jnp.bfloat16)


def up_kernel(x_ref, slab_ref, out_ref):
    copies, height, units = out_ref.shape
    rows = x_ref.shape[1]
    bands, width = slab_ref.shape[0], slab_ref.shape[4]
    total = jnp.zeros((rows, units), jnp.float32)
    squares = jnp.zeros((rows, 1), jnp.float32)
    for band in range(bands):
        x = x_ref[band]
        total += lax.dot_general(
            x[:, :width],
            slab_ref[band, :, 0].reshape(units, width),
            (((1,), (1,)), ((), ())),
            preferred_element_type=jnp.float32,
        )
        squares += jnp.sum(x[:, width:].astype(jnp.float32), axis=1, keepdims=True)
    line = to_lanes(squares, units)
    row = lax.broadcasted_iota(jnp.int32, (height - rows, units), 0)
    tail = jnp.zeros((height - rows, units), jnp.float32)
    for i, term in enumerate(three_terms(line)):
        tail = jnp.where(row == i, term, tail)
    total = total.astype(out_ref.dtype)
    tail = tail.astype(out_ref.dtype)
    for copy in range(copies):
        out_ref[copy, :rows] = total
        out_ref[copy, rows:] = tail


def down_kernel(sums_ref, slab_ref, out_ref):
    bands, rows, width = out_ref.shape
    total = jnp.sum(sums_ref[...].astype(jnp.float32), axis=0)
    squares = jnp.sum(total[rows : rows + 8], axis=0, keepdims=True)
    factor = lax.rsqrt(to_rows(squares, rows) / D + norm_eps)
    upper = jnp.maximum(total[:rows] * factor, 0.0)
    active = (upper * upper).astype(jnp.bfloat16)
    for band in range(bands):
        weights = slab_ref[band, :, 1].reshape(active.shape[1], width)
        out_ref[band] = jnp.dot(active, weights, preferred_element_type=jnp.float32).astype(
            out_ref.dtype
        )


VMEM = pl.BlockSpec(memory_space=pltpu.VMEM)
SMEM = pl.BlockSpec(memory_space=pltpu.SMEM)


def whole(shape):
    return pl.BlockSpec(shape, lambda i: (0,) * len(shape))


def attend(lengths, hidden, squares, gain, out_gain, kv):
    rows, width = hidden.shape
    count = kv.shape[0]
    groups = width // HEAD
    pairs = 2
    block = (2 * pairs,) + kv.shape[1:]
    return pl.pallas_call(
        functools.partial(attend_kernel, pairs),
        grid=(count // (2 * pairs),),
        out_shape=(
            jax.ShapeDtypeStruct((rows, 640), jnp.bfloat16),
            jax.ShapeDtypeStruct((2, rows, 640), jnp.bfloat16),
        ),
        in_specs=[
            SMEM,
            whole(hidden.shape),
            whole(squares.shape),
            whole(gain.shape),
            whole(out_gain.shape),
            pl.BlockSpec(block, lambda i: (i, 0, 0)),
        ],
        out_specs=(whole((rows, 640)), whole((2, rows, 640))),
        scratch_shapes=[
            pltpu.VMEM((rows, width), jnp.float32),
            pltpu.VMEM((groups, rows, HEAD), jnp.float32),
            pltpu.VMEM((groups, rows, HEAD), jnp.float32),
            pltpu.VMEM((rows, HEAD), jnp.float32),
        ],
        compiler_params=pltpu.CompilerParams(vmem_limit_bytes=24 * 1024 * 1024),
    )(lengths, hidden, squares, gain, out_gain, kv)


def body(grad_parts, master, moment1, moment2, kv_cache, hidden_in, attn_gain, ffn_gain, lengths):
    role_index = lax.axis_index("role")
    shards = lax.axis_size("dp")
    tensor = lax.axis_size("tensor")
    bands = tensor // BAND
    bf16 = jnp.bfloat16
    band_groups = [[b * BAND + m for m in range(BAND)] for b in range(bands)]
    member_groups = [[b * BAND + m for b in range(bands)] for m in range(BAND)]
    quarter = master.shape[3]

    grads = grad_parts[0, 0]
    row_count, steps, width = hidden_in.shape
    rows = row_count * steps
    units = master.shape[1]
    wide = 640

    def learn():
        split = pl.pallas_call(
            split_kernel,
            out_shape=jax.ShapeDtypeStruct((shards, units, 2, quarter), bf16),
            in_specs=[pl.BlockSpec(memory_space=pl.ANY)],
            out_specs=VMEM,
            scratch_shapes=[pltpu.SemaphoreType.DMA((shards,))],
        )(grads)
        arriving = lax.all_to_all(split, "dp", 0, 0, tiled=True)
        new_master, blocks = pl.pallas_call(
            adam_kernel,
            out_shape=(
                jax.ShapeDtypeStruct((units, 2, quarter), jnp.float32),
                jax.ShapeDtypeStruct((BAND, 2, units, width), bf16),
            ),
            in_specs=[VMEM] * 4,
            out_specs=(VMEM, VMEM),
            compiler_params=pltpu.CompilerParams(vmem_limit_bytes=24 * 1024 * 1024),
        )(arriving, master[0], moment1[0], moment2[0])
        own = lax.all_to_all(blocks, "tensor", 0, 0, tiled=True, axis_index_groups=band_groups)
        return (
            new_master,
            own,
            jnp.zeros((bands + 2, rows, wide), bf16),
        )

    def roll_out():
        squares = pl.pallas_call(
            squares_kernel,
            out_shape=jax.ShapeDtypeStruct((tensor, 8, 128), jnp.float32),
            in_specs=[VMEM],
            out_specs=VMEM,
        )(hidden_in)
        squares = lax.all_to_all(squares, "tensor", 0, 0, tiled=True)
        hidden = hidden_in.astype(jnp.float32).reshape(rows, width)
        feature_start = lax.axis_index("tensor") * width
        outgoing, halves = attend(
            lengths,
            hidden,
            squares,
            lax.dynamic_slice_in_dim(attn_gain, feature_start, width)[None],
            lax.dynamic_slice_in_dim(ffn_gain, feature_start, width)[None],
            kv_cache[0, :, 0],
        )
        features = lax.all_to_all(
            jnp.broadcast_to(outgoing[None], (bands, rows, wide)),
            "tensor",
            0,
            0,
            tiled=True,
            axis_index_groups=member_groups,
        )
        return (
            jnp.zeros((units, 2, quarter), jnp.float32),
            jnp.zeros((BAND, 2, units, width), bf16),
            jnp.concatenate([features, halves]),
        )

    new_master, own, features = lax.cond(role_index == 0, learn, roll_out)
    features = lax.ppermute(features, "role", [(1, 0)])

    def gather_slabs():
        return lax.all_to_all(
            jnp.broadcast_to(own[None], (shards,) + own.shape), "dp", 0, 0, tiled=True
        )

    def no_slabs():
        return jnp.zeros((shards,) + own.shape, bf16)

    slabs = lax.cond(role_index == 0, gather_slabs, no_slabs)
    slabs, new_master = lax.optimization_barrier((slabs, new_master))
    copied = lax.ppermute(new_master, "role", [(0, 1)]).astype(bf16).astype(jnp.float32)
    weights_after = jnp.where(role_index == 0, new_master, copied)[None]

    sums = pl.pallas_call(
        up_kernel,
        out_shape=jax.ShapeDtypeStruct((BAND, rows + 16, BAND * units), bf16),
        in_specs=[VMEM, VMEM],
        out_specs=VMEM,
    )(features, slabs)
    sums = lax.all_to_all(sums, "tensor", 0, 0, tiled=True, axis_index_groups=band_groups)
    sums, weights_after = lax.optimization_barrier((sums, weights_after))
    parts = pl.pallas_call(
        down_kernel,
        out_shape=jax.ShapeDtypeStruct((bands, rows, width), bf16),
        in_specs=[VMEM, VMEM],
        out_specs=VMEM,
    )(sums, slabs)
    parts = lax.all_to_all(parts, "tensor", 0, 0, tiled=True, axis_index_groups=member_groups)
    middle = jnp.sum(features[bands:, :, :width].astype(jnp.float32), axis=0)
    decoded = (middle + jnp.sum(parts.astype(jnp.float32), axis=0)).astype(bf16)
    decoded = decoded.reshape(row_count, steps, width)
    returned = lax.ppermute(decoded, "role", [(0, 1)])
    return (weights_after, jnp.where(role_index == 0, decoded, returned))


def solution(mesh):
    in_specs = (
        P("role", "dp", "tensor", None, None),
        P("role", "tensor", None, "dp"),
        P("role", "tensor", None, "dp"),
        P("role", "tensor", None, "dp"),
        P("role", "dp", "tensor", None, None),
        P("dp", None, "tensor"),
        P(),
        P(),
        P("dp"),
    )
    out_specs = (P("role", "tensor", None, "dp"), P("dp", None, "tensor"))
    return jax.shard_map(body, mesh=mesh, in_specs=in_specs, out_specs=out_specs, check_vma=False)
```

```python
import functools
import math

import jax
import jax.numpy as jnp
from jax import lax
from jax.experimental import pallas as pl
from jax.experimental.pallas import tpu as pltpu
from jax.sharding import PartitionSpec as P

D = 18432
HEAD = 192
STEPS = 4
BAND = 8


beta_one = 0.9
beta_two = 0.95
rate_factor = 0.5
decay_rate = 0.1
adam_eps = 1e-08
norm_eps = 1e-05
step_count = 10


def adam_update(grad_sum, weights, first, second):
    learn_rate = rate_factor / math.sqrt(D)
    first_new = beta_one * first + (1.0 - beta_one) * grad_sum
    second_new = beta_two * second + (1.0 - beta_two) * grad_sum * grad_sum
    corr_one = 1.0 - beta_one**step_count
    corr_two = 1.0 - beta_two**step_count
    ratio = first_new / corr_one / (jnp.sqrt(second_new / corr_two) + adam_eps)
    return weights - learn_rate * (ratio + decay_rate * weights)


def to_lanes(column, lanes):
    rows = column.shape[0]
    here = lax.broadcasted_iota(jnp.int32, (rows, lanes), 0)
    lane = lax.broadcasted_iota(jnp.int32, (rows, lanes), 1)
    return jnp.sum(jnp.where(here == lane, column, 0.0), axis=0, keepdims=True)


def to_rows(line, rows):
    lanes = line.shape[1]
    here = lax.broadcasted_iota(jnp.int32, (rows, lanes), 0)
    lane = lax.broadcasted_iota(jnp.int32, (rows, lanes), 1)
    return jnp.sum(jnp.where(here == lane, line, 0.0), axis=1, keepdims=True)


def three_terms(values):
    high = values.astype(jnp.bfloat16).astype(jnp.float32)
    middle = (values - high).astype(jnp.bfloat16).astype(jnp.float32)
    return high, middle, values - high - middle


def squares_kernel(hidden_ref, out_ref):
    hidden = hidden_ref[...].astype(jnp.float32)
    squares = jnp.sum(hidden * hidden, axis=2, keepdims=True)
    shape = hidden.shape[:2] + (out_ref.shape[2],)
    row = lax.broadcasted_iota(jnp.int32, shape, 0) * shape[1]
    row = row + lax.broadcasted_iota(jnp.int32, shape, 1)
    lane = lax.broadcasted_iota(jnp.int32, shape, 2)
    line = jnp.sum(jnp.where(lane == row, squares, 0.0), axis=(0, 1))
    out_ref[...] = jnp.broadcast_to(line[None, None], out_ref.shape)


def attend_kernel(
    pairs,
    len_ref,
    hidden_ref,
    squares_ref,
    gain_ref,
    out_gain_ref,
    kv_ref,
    sent_ref,
    halves_ref,
    middle_ref,
    normed_ref,
    hidden_parts_ref,
    flip_normed_ref,
):
    step = pl.program_id(0)
    groups = normed_ref.shape[0]
    rows = hidden_ref.shape[0]
    scale = 1.0 / math.sqrt(HEAD)

    @pl.when(step == 0)
    def _():
        total = jnp.sum(squares_ref[...], axis=0)[0:1]
        factor = lax.rsqrt(to_rows(total, rows) / D + norm_eps)
        hidden = hidden_ref[...]
        normed = hidden * factor * gain_ref[...]
        for q in range(groups):
            part = slice(q * HEAD, (q + 1) * HEAD)
            normed_ref[q] = normed[:, part]
            hidden_parts_ref[q] = hidden[:, part]
        across = lax.broadcasted_iota(jnp.int32, (HEAD, HEAD), 0)
        down = lax.broadcasted_iota(jnp.int32, (HEAD, HEAD), 1)
        reverse = jnp.where(across + down == HEAD - 1, 1.0, 0.0).astype(jnp.bfloat16)
        flip_normed_ref[...] = jnp.dot(
            normed_ref[0].astype(jnp.bfloat16), reverse, preferred_element_type=jnp.float32
        )

    high = lax.broadcasted_iota(jnp.int32, (groups * 8, 1), 0) % 8 >= 4
    row_id = lax.broadcasted_iota(jnp.int32, (groups * 8, 8), 0) % 8
    col_id = lax.broadcasted_iota(jnp.int32, (groups * 8, 8), 1)
    fresh_ok = (row_id // 4 == col_id // 4) & (col_id % 4 <= row_id % 4)
    context = kv_ref.shape[1]
    position = lax.broadcasted_iota(jnp.int32, (groups * 8, context), 1)
    for p in range(pairs):
        pair = step * pairs + p
        first = pl.multiple_of(pair * 8, 8)
        query = jnp.concatenate(
            [normed_ref[q, pl.ds(first, 8), :] for q in range(groups)], axis=0
        ).astype(jnp.bfloat16)
        new_keys = flip_normed_ref[pl.ds(first, 8), :].astype(jnp.bfloat16)
        new_values = normed_ref[1, pl.ds(first, 8), :].astype(jnp.bfloat16)
        contract = (((1,), (1,)), ((), ()))
        scores = []
        for half in range(2):
            keys = kv_ref[2 * p + half, :, :HEAD]
            scores.append(
                lax.dot_general(query, keys, contract, preferred_element_type=jnp.float32)
            )
        cache = jnp.where(high, scores[1], scores[0]) * scale
        length = jnp.where(high, len_ref[2 * pair + 1], len_ref[2 * pair])
        cache = jnp.where(position < length, cache, -jnp.inf)
        fresh = (
            lax.dot_general(query, new_keys, contract, preferred_element_type=jnp.float32)
            * scale
        )
        fresh = jnp.where(fresh_ok, fresh, -jnp.inf)
        top = jnp.maximum(
            jnp.max(cache, axis=1, keepdims=True), jnp.max(fresh, axis=1, keepdims=True)
        )
        cache = jnp.exp(cache - top)
        fresh = jnp.exp(fresh - top)
        total = jnp.sum(cache, axis=1, keepdims=True) + jnp.sum(fresh, axis=1, keepdims=True)
        cache = (cache / total).astype(jnp.bfloat16)
        fresh = (fresh / total).astype(jnp.bfloat16)
        weighed = []
        for half in range(2):
            values = kv_ref[2 * p + half, :, HEAD:]
            weighed.append(jnp.dot(cache, values, preferred_element_type=jnp.float32))
        attended = jnp.where(high, weighed[1], weighed[0]) + jnp.dot(
            fresh, new_values, preferred_element_type=jnp.float32
        )
        for q in range(groups):
            middle_ref[pl.ds(first, 8), q * HEAD : (q + 1) * HEAD] = (
                hidden_parts_ref[q, pl.ds(first, 8), :] + attended[q * 8 : (q + 1) * 8]
            )

    @pl.when(step == pl.num_programs(0) - 1)
    def _():
        middle = middle_ref[...]
        width = middle.shape[1]
        squares = jnp.sum(middle * middle, axis=1, keepdims=True)
        lane = lax.broadcasted_iota(jnp.int32, (rows, sent_ref.shape[1] - width), 1)
        tail = jnp.zeros(lane.shape, jnp.float32)
        for i, term in enumerate(three_terms(squares)):
            tail = jnp.where(lane == i, term, tail)
        sent_ref[:, :width] = (middle * out_gain_ref[...]).astype(jnp.bfloat16)
        sent_ref[:, width:] = tail.astype(jnp.bfloat16)
        rounded = middle.astype(jnp.bfloat16)
        halves_ref[0, :, :width] = rounded
        halves_ref[1, :, :width] = (middle - rounded.astype(jnp.float32)).astype(jnp.bfloat16)
        halves_ref[:, :, width:] = jnp.zeros((2,) + lane.shape, jnp.bfloat16)


def split_kernel(grads_ref, out_ref, sems):
    quarter = out_ref.shape[3]
    copies = [
        pltpu.make_async_copy(
            grads_ref.at[:, :, pl.ds(k * quarter, quarter)], out_ref.at[k], sems.at[k]
        )
        for k in range(out_ref.shape[0])
    ]
    for copy in copies:
        copy.start()
    for copy in copies:
        copy.wait()


def adam_kernel(grads_ref, w_ref, m1_ref, m2_ref, new_ref, blocks_ref):
    members, halves, units, width = blocks_ref.shape
    step = 2 * width
    for half in range(halves):
        for i in range(members // 2):
            cut = slice(i * step, (i + 1) * step)
            grad_sum = jnp.sum(grads_ref[:, :, half, cut].astype(jnp.float32), axis=0)
            new = adam_update(
                grad_sum, w_ref[:, half, cut], m1_ref[:, half, cut], m2_ref[:, half, cut]
            )
            new_ref[:, half, cut] = new
            blocks_ref[2 * i, half] = new[:, :width].astype(jnp.bfloat16)
            blocks_ref[2 * i + 1, half] = new[:, width:].astype(jnp.bfloat16)


def up_kernel(x_ref, slab_ref, out_ref):
    copies, height, units = out_ref.shape
    rows = x_ref.shape[1]
    bands, width = slab_ref.shape[0], slab_ref.shape[4]
    total = jnp.zeros((rows, units), jnp.float32)
    squares = jnp.zeros((rows, 1), jnp.float32)
    for band in range(bands):
        x = x_ref[band]
        total += lax.dot_general(
            x[:, :width],
            slab_ref[band, :, 0].reshape(units, width),
            (((1,), (1,)), ((), ())),
            preferred_element_type=jnp.float32,
        )
        squares += jnp.sum(x[:, width:].astype(jnp.float32), axis=1, keepdims=True)
    line = to_lanes(squares, units)
    row = lax.broadcasted_iota(jnp.int32, (height - rows, units), 0)
    tail = jnp.zeros((height - rows, units), jnp.float32)
    for i, term in enumerate(three_terms(line)):
        tail = jnp.where(row == i, term, tail)
    total = total.astype(out_ref.dtype)
    tail = tail.astype(out_ref.dtype)
    for copy in range(copies):
        out_ref[copy, :rows] = total
        out_ref[copy, rows:] = tail


def down_kernel(sums_ref, slab_ref, out_ref):
    bands, rows, width = out_ref.shape
    total = jnp.sum(sums_ref[...].astype(jnp.float32), axis=0)
    squares = jnp.sum(total[rows : rows + 8], axis=0, keepdims=True)
    factor = lax.rsqrt(to_rows(squares, rows) / D + norm_eps)
    upper = jnp.maximum(total[:rows] * factor, 0.0)
    active = (upper * upper).astype(jnp.bfloat16)
    for band in range(bands):
        weights = slab_ref[band, :, 1].reshape(active.shape[1], width)
        out_ref[band] = jnp.dot(active, weights, preferred_element_type=jnp.float32).astype(
            out_ref.dtype
        )


VMEM = pl.BlockSpec(memory_space=pltpu.VMEM)
SMEM = pl.BlockSpec(memory_space=pltpu.SMEM)


def whole(shape):
    return pl.BlockSpec(shape, lambda i: (0,) * len(shape))


def attend(lengths, hidden, squares, gain, out_gain, kv):
    rows, width = hidden.shape
    count = kv.shape[0]
    groups = width // HEAD
    pairs = 2
    block = (2 * pairs,) + kv.shape[1:]
    return pl.pallas_call(
        functools.partial(attend_kernel, pairs),
        grid=(count // (2 * pairs),),
        out_shape=(
            jax.ShapeDtypeStruct((rows, 640), jnp.bfloat16),
            jax.ShapeDtypeStruct((2, rows, 640), jnp.bfloat16),
        ),
        in_specs=[
            SMEM,
            whole(hidden.shape),
            whole(squares.shape),
            whole(gain.shape),
            whole(out_gain.shape),
            pl.BlockSpec(block, lambda i: (i, 0, 0)),
        ],
        out_specs=(whole((rows, 640)), whole((2, rows, 640))),
        scratch_shapes=[
            pltpu.VMEM((rows, width), jnp.float32),
            pltpu.VMEM((groups, rows, HEAD), jnp.float32),
            pltpu.VMEM((groups, rows, HEAD), jnp.float32),
            pltpu.VMEM((rows, HEAD), jnp.float32),
        ],
        compiler_params=pltpu.CompilerParams(vmem_limit_bytes=24 * 1024 * 1024),
    )(lengths, hidden, squares, gain, out_gain, kv)


def body(grad_parts, master, moment1, moment2, kv_cache, hidden_in, attn_gain, ffn_gain, lengths):
    role_index = lax.axis_index("role")
    shards = lax.axis_size("dp")
    tensor = lax.axis_size("tensor")
    bands = tensor // BAND
    bf16 = jnp.bfloat16
    band_groups = [[b * BAND + m for m in range(BAND)] for b in range(bands)]
    member_groups = [[b * BAND + m for b in range(bands)] for m in range(BAND)]
    quarter = master.shape[3]

    grads = grad_parts[0, 0]
    row_count, steps, width = hidden_in.shape
    rows = row_count * steps
    units = master.shape[1]
    wide = 640

    def learn():
        split = pl.pallas_call(
            split_kernel,
            out_shape=jax.ShapeDtypeStruct((shards, units, 2, quarter), bf16),
            in_specs=[pl.BlockSpec(memory_space=pl.ANY)],
            out_specs=VMEM,
            scratch_shapes=[pltpu.SemaphoreType.DMA((shards,))],
            compiler_params=pltpu.CompilerParams(vmem_limit_bytes=16 * 1024 * 1024),
        )(grads)
        arriving = lax.all_to_all(split, "dp", 0, 0, tiled=True)
        new_master, blocks = pl.pallas_call(
            adam_kernel,
            out_shape=(
                jax.ShapeDtypeStruct((units, 2, quarter), jnp.float32),
                jax.ShapeDtypeStruct((BAND, 2, units, width), bf16),
            ),
            in_specs=[VMEM] * 4,
            out_specs=(VMEM, VMEM),
            compiler_params=pltpu.CompilerParams(vmem_limit_bytes=24 * 1024 * 1024),
        )(arriving, master[0], moment1[0], moment2[0])
        own = lax.all_to_all(blocks, "tensor", 0, 0, tiled=True, axis_index_groups=band_groups)
        return (
            new_master,
            own,
            jnp.zeros((bands + 2, rows, wide), bf16),
        )

    def roll_out():
        squares = pl.pallas_call(
            squares_kernel,
            out_shape=jax.ShapeDtypeStruct((tensor, 8, 128), jnp.float32),
            in_specs=[VMEM],
            out_specs=VMEM,
            compiler_params=pltpu.CompilerParams(vmem_limit_bytes=16 * 1024 * 1024),
        )(hidden_in)
        squares = lax.all_to_all(squares, "tensor", 0, 0, tiled=True)
        hidden = hidden_in.astype(jnp.float32).reshape(rows, width)
        feature_start = lax.axis_index("tensor") * width
        outgoing, halves = attend(
            lengths,
            hidden,
            squares,
            lax.dynamic_slice_in_dim(attn_gain, feature_start, width)[None],
            lax.dynamic_slice_in_dim(ffn_gain, feature_start, width)[None],
            kv_cache[0, :, 0],
        )
        features = lax.all_to_all(
            jnp.broadcast_to(outgoing[None], (bands, rows, wide)),
            "tensor",
            0,
            0,
            tiled=True,
            axis_index_groups=member_groups,
        )
        return (
            jnp.zeros((units, 2, quarter), jnp.float32),
            jnp.zeros((BAND, 2, units, width), bf16),
            jnp.concatenate([features, halves]),
        )

    new_master, own, features = lax.cond(role_index == 0, learn, roll_out)
    features = lax.ppermute(features, "role", [(1, 0)])

    def gather_slabs():
        return lax.all_to_all(
            jnp.broadcast_to(own[None], (shards,) + own.shape), "dp", 0, 0, tiled=True
        )

    def no_slabs():
        return jnp.zeros((shards,) + own.shape, bf16)

    slabs = lax.cond(role_index == 0, gather_slabs, no_slabs)
    slabs, new_master = lax.optimization_barrier((slabs, new_master))
    copied = lax.ppermute(new_master, "role", [(0, 1)]).astype(bf16).astype(jnp.float32)
    weights_after = jnp.where(role_index == 0, new_master, copied)[None]

    sums = pl.pallas_call(
        up_kernel,
        out_shape=jax.ShapeDtypeStruct((BAND, rows + 16, BAND * units), bf16),
        in_specs=[VMEM, VMEM],
        out_specs=VMEM,
        compiler_params=pltpu.CompilerParams(vmem_limit_bytes=16 * 1024 * 1024),
    )(features, slabs)
    sums = lax.all_to_all(sums, "tensor", 0, 0, tiled=True, axis_index_groups=band_groups)
    sums, weights_after = lax.optimization_barrier((sums, weights_after))
    parts = pl.pallas_call(
        down_kernel,
        out_shape=jax.ShapeDtypeStruct((bands, rows, width), bf16),
        in_specs=[VMEM, VMEM],
        out_specs=VMEM,
        compiler_params=pltpu.CompilerParams(vmem_limit_bytes=16 * 1024 * 1024),
    )(sums, slabs)
    parts = lax.all_to_all(parts, "tensor", 0, 0, tiled=True, axis_index_groups=member_groups)
    middle = jnp.sum(features[bands:, :, :width].astype(jnp.float32), axis=0)
    decoded = (middle + jnp.sum(parts.astype(jnp.float32), axis=0)).astype(bf16)
    decoded = decoded.reshape(row_count, steps, width)
    returned = lax.ppermute(decoded, "role", [(0, 1)])
    return (weights_after, jnp.where(role_index == 0, decoded, returned))


def solution(mesh):
    in_specs = (
        P("role", "dp", "tensor", None, None),
        P("role", "tensor", None, "dp"),
        P("role", "tensor", None, "dp"),
        P("role", "tensor", None, "dp"),
        P("role", "dp", "tensor", None, None),
        P("dp", None, "tensor"),
        P(),
        P(),
        P("dp"),
    )
    out_specs = (P("role", "tensor", None, "dp"), P("dp", None, "tensor"))
    return jax.shard_map(body, mesh=mesh, in_specs=in_specs, out_specs=out_specs, check_vma=False)
```

```python
import functools
import math

import jax
import jax.numpy as jnp
from jax import lax
from jax.experimental import pallas as pl
from jax.experimental.pallas import tpu as pltpu
from jax.sharding import PartitionSpec as P

D = 18432
HEAD = 192
STEPS = 4
BAND = 8


beta_one = 0.9
beta_two = 0.95
rate_factor = 0.5
decay_rate = 0.1
adam_eps = 1e-08
norm_eps = 1e-05
step_count = 10


def adam_update(grad_sum, weights, first, second):
    learn_rate = rate_factor / math.sqrt(D)
    first_new = beta_one * first + (1.0 - beta_one) * grad_sum
    second_new = beta_two * second + (1.0 - beta_two) * grad_sum * grad_sum
    corr_one = 1.0 - beta_one**step_count
    corr_two = 1.0 - beta_two**step_count
    ratio = first_new / corr_one / (jnp.sqrt(second_new / corr_two) + adam_eps)
    return weights - learn_rate * (ratio + decay_rate * weights)


def to_lanes(column, lanes):
    rows = column.shape[0]
    here = lax.broadcasted_iota(jnp.int32, (rows, lanes), 0)
    lane = lax.broadcasted_iota(jnp.int32, (rows, lanes), 1)
    return jnp.sum(jnp.where(here == lane, column, 0.0), axis=0, keepdims=True)


def to_rows(line, rows):
    lanes = line.shape[1]
    here = lax.broadcasted_iota(jnp.int32, (rows, lanes), 0)
    lane = lax.broadcasted_iota(jnp.int32, (rows, lanes), 1)
    return jnp.sum(jnp.where(here == lane, line, 0.0), axis=1, keepdims=True)


def three_terms(values):
    high = values.astype(jnp.bfloat16).astype(jnp.float32)
    middle = (values - high).astype(jnp.bfloat16).astype(jnp.float32)
    return high, middle, values - high - middle


def squares_kernel(hidden_ref, out_ref):
    hidden = hidden_ref[...].astype(jnp.float32)
    squares = jnp.sum(hidden * hidden, axis=2, keepdims=True)
    shape = hidden.shape[:2] + (out_ref.shape[2],)
    row = lax.broadcasted_iota(jnp.int32, shape, 0) * shape[1]
    row = row + lax.broadcasted_iota(jnp.int32, shape, 1)
    lane = lax.broadcasted_iota(jnp.int32, shape, 2)
    line = jnp.sum(jnp.where(lane == row, squares, 0.0), axis=(0, 1))
    out_ref[...] = jnp.broadcast_to(line[None, None], out_ref.shape)


def attend_kernel(
    pairs,
    len_ref,
    hidden_ref,
    squares_ref,
    gain_ref,
    out_gain_ref,
    kv_ref,
    sent_ref,
    halves_ref,
    middle_ref,
    normed_ref,
    hidden_parts_ref,
    flip_normed_ref,
):
    step = pl.program_id(0)
    groups = normed_ref.shape[0]
    rows = hidden_ref.shape[0]
    scale = 1.0 / math.sqrt(HEAD)

    @pl.when(step == 0)
    def _():
        total = jnp.sum(squares_ref[...], axis=0)[0:1]
        factor = lax.rsqrt(to_rows(total, rows) / D + norm_eps)
        hidden = hidden_ref[...]
        normed = hidden * factor * gain_ref[...]
        for q in range(groups):
            part = slice(q * HEAD, (q + 1) * HEAD)
            normed_ref[q] = normed[:, part]
            hidden_parts_ref[q] = hidden[:, part]
        across = lax.broadcasted_iota(jnp.int32, (HEAD, HEAD), 0)
        down = lax.broadcasted_iota(jnp.int32, (HEAD, HEAD), 1)
        reverse = jnp.where(across + down == HEAD - 1, 1.0, 0.0).astype(jnp.bfloat16)
        flip_normed_ref[...] = jnp.dot(
            normed_ref[0].astype(jnp.bfloat16), reverse, preferred_element_type=jnp.float32
        )

    high = lax.broadcasted_iota(jnp.int32, (groups * 8, 1), 0) % 8 >= 4
    row_id = lax.broadcasted_iota(jnp.int32, (groups * 8, 8), 0) % 8
    col_id = lax.broadcasted_iota(jnp.int32, (groups * 8, 8), 1)
    fresh_ok = (row_id // 4 == col_id // 4) & (col_id % 4 <= row_id % 4)
    context = kv_ref.shape[1]
    position = lax.broadcasted_iota(jnp.int32, (groups * 8, context), 1)
    for p in range(pairs):
        pair = step * pairs + p
        first = pl.multiple_of(pair * 8, 8)
        query = jnp.concatenate(
            [normed_ref[q, pl.ds(first, 8), :] for q in range(groups)], axis=0
        ).astype(jnp.bfloat16)
        new_keys = flip_normed_ref[pl.ds(first, 8), :].astype(jnp.bfloat16)
        new_values = normed_ref[1, pl.ds(first, 8), :].astype(jnp.bfloat16)
        contract = (((1,), (1,)), ((), ()))
        scores = []
        for half in range(2):
            keys = kv_ref[2 * p + half, :, :HEAD]
            scores.append(
                lax.dot_general(query, keys, contract, preferred_element_type=jnp.float32)
            )
        cache = jnp.where(high, scores[1], scores[0]) * scale
        length = jnp.where(high, len_ref[2 * pair + 1], len_ref[2 * pair])
        cache = jnp.where(position < length, cache, -jnp.inf)
        fresh = (
            lax.dot_general(query, new_keys, contract, preferred_element_type=jnp.float32)
            * scale
        )
        fresh = jnp.where(fresh_ok, fresh, -jnp.inf)
        top = jnp.maximum(
            jnp.max(cache, axis=1, keepdims=True), jnp.max(fresh, axis=1, keepdims=True)
        )
        cache = jnp.exp(cache - top)
        fresh = jnp.exp(fresh - top)
        total = jnp.sum(cache, axis=1, keepdims=True) + jnp.sum(fresh, axis=1, keepdims=True)
        cache = (cache / total).astype(jnp.bfloat16)
        fresh = (fresh / total).astype(jnp.bfloat16)
        weighed = []
        for half in range(2):
            values = kv_ref[2 * p + half, :, HEAD:]
            weighed.append(jnp.dot(cache, values, preferred_element_type=jnp.float32))
        attended = jnp.where(high, weighed[1], weighed[0]) + jnp.dot(
            fresh, new_values, preferred_element_type=jnp.float32
        )
        for q in range(groups):
            middle_ref[pl.ds(first, 8), q * HEAD : (q + 1) * HEAD] = (
                hidden_parts_ref[q, pl.ds(first, 8), :] + attended[q * 8 : (q + 1) * 8]
            )

    @pl.when(step == pl.num_programs(0) - 1)
    def _():
        middle = middle_ref[...]
        width = middle.shape[1]
        squares = jnp.sum(middle * middle, axis=1, keepdims=True)
        lane = lax.broadcasted_iota(jnp.int32, (rows, sent_ref.shape[1] - width), 1)
        tail = jnp.zeros(lane.shape, jnp.float32)
        for i, term in enumerate(three_terms(squares)):
            tail = jnp.where(lane == i, term, tail)
        sent_ref[:, :width] = (middle * out_gain_ref[...]).astype(jnp.bfloat16)
        sent_ref[:, width:] = tail.astype(jnp.bfloat16)
        rounded = middle.astype(jnp.bfloat16)
        halves_ref[0, :, :width] = rounded
        halves_ref[1, :, :width] = (middle - rounded.astype(jnp.float32)).astype(jnp.bfloat16)
        halves_ref[:, :, width:] = jnp.zeros((2,) + lane.shape, jnp.bfloat16)


def split_kernel(grads_ref, out_ref, sems):
    quarter = out_ref.shape[3]
    copies = [
        pltpu.make_async_copy(
            grads_ref.at[:, :, pl.ds(k * quarter, quarter)], out_ref.at[k], sems.at[k]
        )
        for k in range(out_ref.shape[0])
    ]
    for copy in copies:
        copy.start()
    for copy in copies:
        copy.wait()


def adam_kernel(grads_ref, w_ref, m1_ref, m2_ref, new_ref, blocks_ref):
    members, _, double = blocks_ref.shape
    width = double // 2
    for half in range(2):
        for i in range(members // 2):
            cut = slice(i * double, (i + 1) * double)
            grad_sum = jnp.sum(grads_ref[:, :, half, cut].astype(jnp.float32), axis=0)
            new = adam_update(
                grad_sum, w_ref[:, half, cut], m1_ref[:, half, cut], m2_ref[:, half, cut]
            )
            new_ref[:, half, cut] = new
            place = slice(half * width, (half + 1) * width)
            blocks_ref[2 * i, :, place] = new[:, :width].astype(jnp.bfloat16)
            blocks_ref[2 * i + 1, :, place] = new[:, width:].astype(jnp.bfloat16)


def up_kernel(x_ref, slab_ref, out_ref):
    copies, height, units = out_ref.shape
    rows = x_ref.shape[1]
    bands, width = slab_ref.shape[0], slab_ref.shape[3] // 2
    total = jnp.zeros((rows, units), jnp.float32)
    squares = jnp.zeros((rows, 1), jnp.float32)
    for band in range(bands):
        x = x_ref[band]
        total += lax.dot_general(
            x[:, :width],
            slab_ref[band, :, :, :width].reshape(units, width),
            (((1,), (1,)), ((), ())),
            preferred_element_type=jnp.float32,
        )
        squares += jnp.sum(x[:, width:].astype(jnp.float32), axis=1, keepdims=True)
    line = to_lanes(squares, units)
    row = lax.broadcasted_iota(jnp.int32, (height - rows, units), 0)
    tail = jnp.zeros((height - rows, units), jnp.float32)
    for i, term in enumerate(three_terms(line)):
        tail = jnp.where(row == i, term, tail)
    total = total.astype(out_ref.dtype)
    tail = tail.astype(out_ref.dtype)
    for copy in range(copies):
        out_ref[copy, :rows] = total
        out_ref[copy, rows:] = tail


def down_kernel(sums_ref, slab_ref, out_ref):
    bands, rows, width = out_ref.shape
    total = jnp.sum(sums_ref[...].astype(jnp.float32), axis=0)
    squares = jnp.sum(total[rows : rows + 8], axis=0, keepdims=True)
    factor = lax.rsqrt(to_rows(squares, rows) / D + norm_eps)
    upper = jnp.maximum(total[:rows] * factor, 0.0)
    active = (upper * upper).astype(jnp.bfloat16)
    for band in range(bands):
        weights = slab_ref[band, :, :, width:].reshape(active.shape[1], width)
        out_ref[band] = jnp.dot(active, weights, preferred_element_type=jnp.float32).astype(
            out_ref.dtype
        )


VMEM = pl.BlockSpec(memory_space=pltpu.VMEM)
SMEM = pl.BlockSpec(memory_space=pltpu.SMEM)


def whole(shape):
    return pl.BlockSpec(shape, lambda i: (0,) * len(shape))


def attend(lengths, hidden, squares, gain, out_gain, kv):
    rows, width = hidden.shape
    count = kv.shape[0]
    groups = width // HEAD
    pairs = 2
    block = (2 * pairs,) + kv.shape[1:]
    return pl.pallas_call(
        functools.partial(attend_kernel, pairs),
        grid=(count // (2 * pairs),),
        out_shape=(
            jax.ShapeDtypeStruct((rows, 640), jnp.bfloat16),
            jax.ShapeDtypeStruct((2, rows, 640), jnp.bfloat16),
        ),
        in_specs=[
            SMEM,
            whole(hidden.shape),
            whole(squares.shape),
            whole(gain.shape),
            whole(out_gain.shape),
            pl.BlockSpec(block, lambda i: (i, 0, 0)),
        ],
        out_specs=(whole((rows, 640)), whole((2, rows, 640))),
        scratch_shapes=[
            pltpu.VMEM((rows, width), jnp.float32),
            pltpu.VMEM((groups, rows, HEAD), jnp.float32),
            pltpu.VMEM((groups, rows, HEAD), jnp.float32),
            pltpu.VMEM((rows, HEAD), jnp.float32),
        ],
        compiler_params=pltpu.CompilerParams(vmem_limit_bytes=24 * 1024 * 1024),
    )(lengths, hidden, squares, gain, out_gain, kv)


def body(grad_parts, master, moment1, moment2, kv_cache, hidden_in, attn_gain, ffn_gain, lengths):
    role_index = lax.axis_index("role")
    shards = lax.axis_size("dp")
    tensor = lax.axis_size("tensor")
    bands = tensor // BAND
    bf16 = jnp.bfloat16
    band_groups = [[b * BAND + m for m in range(BAND)] for b in range(bands)]
    member_groups = [[b * BAND + m for b in range(bands)] for m in range(BAND)]
    quarter = master.shape[3]

    grads = grad_parts[0, 0]
    row_count, steps, width = hidden_in.shape
    rows = row_count * steps
    units = master.shape[1]
    wide = 640

    def learn():
        split = pl.pallas_call(
            split_kernel,
            out_shape=jax.ShapeDtypeStruct((shards, units, 2, quarter), bf16),
            in_specs=[pl.BlockSpec(memory_space=pl.ANY)],
            out_specs=VMEM,
            scratch_shapes=[pltpu.SemaphoreType.DMA((shards,))],
            compiler_params=pltpu.CompilerParams(vmem_limit_bytes=16 * 1024 * 1024),
        )(grads)
        arriving = lax.all_to_all(split, "dp", 0, 0, tiled=True)
        new_master, blocks = pl.pallas_call(
            adam_kernel,
            out_shape=(
                jax.ShapeDtypeStruct((units, 2, quarter), jnp.float32),
                jax.ShapeDtypeStruct((BAND, units, 2 * width), bf16),
            ),
            in_specs=[VMEM] * 4,
            out_specs=(VMEM, VMEM),
            compiler_params=pltpu.CompilerParams(vmem_limit_bytes=24 * 1024 * 1024),
        )(arriving, master[0], moment1[0], moment2[0])
        own = lax.all_to_all(blocks, "tensor", 0, 0, tiled=True, axis_index_groups=band_groups)
        return (
            new_master,
            own,
            jnp.zeros((bands + 2, rows, wide), bf16),
        )

    def roll_out():
        squares = pl.pallas_call(
            squares_kernel,
            out_shape=jax.ShapeDtypeStruct((tensor, 8, 128), jnp.float32),
            in_specs=[VMEM],
            out_specs=VMEM,
            compiler_params=pltpu.CompilerParams(vmem_limit_bytes=16 * 1024 * 1024),
        )(hidden_in)
        squares = lax.all_to_all(squares, "tensor", 0, 0, tiled=True)
        hidden = hidden_in.astype(jnp.float32).reshape(rows, width)
        feature_start = lax.axis_index("tensor") * width
        outgoing, halves = attend(
            lengths,
            hidden,
            squares,
            lax.dynamic_slice_in_dim(attn_gain, feature_start, width)[None],
            lax.dynamic_slice_in_dim(ffn_gain, feature_start, width)[None],
            kv_cache[0, :, 0],
        )
        features = lax.all_to_all(
            jnp.broadcast_to(outgoing[None], (bands, rows, wide)),
            "tensor",
            0,
            0,
            tiled=True,
            axis_index_groups=member_groups,
        )
        return (
            jnp.zeros((units, 2, quarter), jnp.float32),
            jnp.zeros((BAND, units, 2 * width), bf16),
            jnp.concatenate([features, halves]),
        )

    new_master, own, features = lax.cond(role_index == 0, learn, roll_out)
    features = lax.ppermute(features, "role", [(1, 0)])

    def gather_slabs():
        return lax.all_to_all(
            jnp.broadcast_to(own[None], (shards,) + own.shape), "dp", 0, 0, tiled=True
        )

    def no_slabs():
        return jnp.zeros((shards,) + own.shape, bf16)

    slabs = lax.cond(role_index == 0, gather_slabs, no_slabs)
    sums = pl.pallas_call(
        up_kernel,
        out_shape=jax.ShapeDtypeStruct((BAND, rows + 16, BAND * units), bf16),
        in_specs=[VMEM, VMEM],
        out_specs=VMEM,
        compiler_params=pltpu.CompilerParams(vmem_limit_bytes=16 * 1024 * 1024),
    )(features, slabs)
    sums, new_master = lax.optimization_barrier((sums, new_master))
    copied = lax.ppermute(new_master, "role", [(0, 1)]).astype(bf16).astype(jnp.float32)
    weights_after = jnp.where(role_index == 0, new_master, copied)[None]
    sums = lax.all_to_all(sums, "tensor", 0, 0, tiled=True, axis_index_groups=band_groups)
    sums, weights_after = lax.optimization_barrier((sums, weights_after))
    parts = pl.pallas_call(
        down_kernel,
        out_shape=jax.ShapeDtypeStruct((bands, rows, width), bf16),
        in_specs=[VMEM, VMEM],
        out_specs=VMEM,
        compiler_params=pltpu.CompilerParams(vmem_limit_bytes=16 * 1024 * 1024),
    )(sums, slabs)
    parts = lax.all_to_all(parts, "tensor", 0, 0, tiled=True, axis_index_groups=member_groups)
    middle = jnp.sum(features[bands:, :, :width].astype(jnp.float32), axis=0)
    decoded = (middle + jnp.sum(parts.astype(jnp.float32), axis=0)).astype(bf16)
    decoded = decoded.reshape(row_count, steps, width)
    returned = lax.ppermute(decoded, "role", [(0, 1)])
    return (weights_after, jnp.where(role_index == 0, decoded, returned))


def solution(mesh):
    in_specs = (
        P("role", "dp", "tensor", None, None),
        P("role", "tensor", None, "dp"),
        P("role", "tensor", None, "dp"),
        P("role", "tensor", None, "dp"),
        P("role", "dp", "tensor", None, None),
        P("dp", None, "tensor"),
        P(),
        P(),
        P("dp"),
    )
    out_specs = (P("role", "tensor", None, "dp"), P("dp", None, "tensor"))
    return jax.shard_map(body, mesh=mesh, in_specs=in_specs, out_specs=out_specs, check_vma=False)
```

```python
import functools
import math

import jax
import jax.numpy as jnp
from jax import lax
from jax.experimental import pallas as pl
from jax.experimental.pallas import tpu as pltpu
from jax.sharding import PartitionSpec as P

D = 18432
HEAD = 192
STEPS = 4
BAND = 8


beta_one = 0.9
beta_two = 0.95
rate_factor = 0.5
decay_rate = 0.1
adam_eps = 1e-08
norm_eps = 1e-05
step_count = 10


def adam_update(grad_sum, weights, first, second):
    learn_rate = rate_factor / math.sqrt(D)
    first_new = beta_one * first + (1.0 - beta_one) * grad_sum
    second_new = beta_two * second + (1.0 - beta_two) * grad_sum * grad_sum
    corr_one = 1.0 - beta_one**step_count
    corr_two = 1.0 - beta_two**step_count
    ratio = first_new / corr_one / (jnp.sqrt(second_new / corr_two) + adam_eps)
    return weights - learn_rate * (ratio + decay_rate * weights)


def to_lanes(column, lanes):
    rows = column.shape[0]
    here = lax.broadcasted_iota(jnp.int32, (rows, lanes), 0)
    lane = lax.broadcasted_iota(jnp.int32, (rows, lanes), 1)
    return jnp.sum(jnp.where(here == lane, column, 0.0), axis=0, keepdims=True)


def to_rows(line, rows):
    lanes = line.shape[1]
    here = lax.broadcasted_iota(jnp.int32, (rows, lanes), 0)
    lane = lax.broadcasted_iota(jnp.int32, (rows, lanes), 1)
    return jnp.sum(jnp.where(here == lane, line, 0.0), axis=1, keepdims=True)


def three_terms(values):
    high = values.astype(jnp.bfloat16).astype(jnp.float32)
    middle = (values - high).astype(jnp.bfloat16).astype(jnp.float32)
    return high, middle, values - high - middle


def squares_kernel(hidden_ref, out_ref):
    hidden = hidden_ref[...].astype(jnp.float32)
    squares = jnp.sum(hidden * hidden, axis=2, keepdims=True)
    shape = hidden.shape[:2] + (out_ref.shape[2],)
    row = lax.broadcasted_iota(jnp.int32, shape, 0) * shape[1]
    row = row + lax.broadcasted_iota(jnp.int32, shape, 1)
    lane = lax.broadcasted_iota(jnp.int32, shape, 2)
    line = jnp.sum(jnp.where(lane == row, squares, 0.0), axis=(0, 1))
    out_ref[...] = jnp.broadcast_to(line[None, None], out_ref.shape)


def attend_kernel(
    pairs,
    len_ref,
    hidden_ref,
    squares_ref,
    gain_ref,
    out_gain_ref,
    kv_ref,
    sent_ref,
    halves_ref,
    middle_ref,
    normed_ref,
    hidden_parts_ref,
    flip_normed_ref,
):
    step = pl.program_id(0)
    groups = normed_ref.shape[0]
    rows = hidden_ref.shape[0]
    scale = 1.0 / math.sqrt(HEAD)

    @pl.when(step == 0)
    def _():
        total = jnp.sum(squares_ref[...], axis=0)[0:1]
        factor = lax.rsqrt(to_rows(total, rows) / D + norm_eps)
        hidden = hidden_ref[...]
        normed = hidden * factor * gain_ref[...]
        for q in range(groups):
            part = slice(q * HEAD, (q + 1) * HEAD)
            normed_ref[q] = normed[:, part]
            hidden_parts_ref[q] = hidden[:, part]
        across = lax.broadcasted_iota(jnp.int32, (HEAD, HEAD), 0)
        down = lax.broadcasted_iota(jnp.int32, (HEAD, HEAD), 1)
        reverse = jnp.where(across + down == HEAD - 1, 1.0, 0.0).astype(jnp.bfloat16)
        flip_normed_ref[...] = jnp.dot(
            normed_ref[0].astype(jnp.bfloat16), reverse, preferred_element_type=jnp.float32
        )

    high = lax.broadcasted_iota(jnp.int32, (groups * 8, 1), 0) % 8 >= 4
    row_id = lax.broadcasted_iota(jnp.int32, (groups * 8, 8), 0) % 8
    col_id = lax.broadcasted_iota(jnp.int32, (groups * 8, 8), 1)
    fresh_ok = (row_id // 4 == col_id // 4) & (col_id % 4 <= row_id % 4)
    context = kv_ref.shape[1]
    position = lax.broadcasted_iota(jnp.int32, (groups * 8, context), 1)
    for p in range(pairs):
        pair = step * pairs + p
        first = pl.multiple_of(pair * 8, 8)
        query = jnp.concatenate(
            [normed_ref[q, pl.ds(first, 8), :] for q in range(groups)], axis=0
        ).astype(jnp.bfloat16)
        new_keys = flip_normed_ref[pl.ds(first, 8), :].astype(jnp.bfloat16)
        new_values = normed_ref[1, pl.ds(first, 8), :].astype(jnp.bfloat16)
        contract = (((1,), (1,)), ((), ()))
        scores = []
        for half in range(2):
            keys = kv_ref[2 * p + half, :, :HEAD]
            scores.append(
                lax.dot_general(query, keys, contract, preferred_element_type=jnp.float32)
            )
        cache = jnp.where(high, scores[1], scores[0]) * scale
        length = jnp.where(high, len_ref[2 * pair + 1], len_ref[2 * pair])
        cache = jnp.where(position < length, cache, -jnp.inf)
        fresh = (
            lax.dot_general(query, new_keys, contract, preferred_element_type=jnp.float32)
            * scale
        )
        fresh = jnp.where(fresh_ok, fresh, -jnp.inf)
        top = jnp.maximum(
            jnp.max(cache, axis=1, keepdims=True), jnp.max(fresh, axis=1, keepdims=True)
        )
        cache = jnp.exp(cache - top)
        fresh = jnp.exp(fresh - top)
        total = jnp.sum(cache, axis=1, keepdims=True) + jnp.sum(fresh, axis=1, keepdims=True)
        cache = (cache / total).astype(jnp.bfloat16)
        fresh = (fresh / total).astype(jnp.bfloat16)
        weighed = []
        for half in range(2):
            values = kv_ref[2 * p + half, :, HEAD:]
            weighed.append(jnp.dot(cache, values, preferred_element_type=jnp.float32))
        attended = jnp.where(high, weighed[1], weighed[0]) + jnp.dot(
            fresh, new_values, preferred_element_type=jnp.float32
        )
        for q in range(groups):
            middle_ref[pl.ds(first, 8), q * HEAD : (q + 1) * HEAD] = (
                hidden_parts_ref[q, pl.ds(first, 8), :] + attended[q * 8 : (q + 1) * 8]
            )

    @pl.when(step == pl.num_programs(0) - 1)
    def _():
        middle = middle_ref[...]
        width = middle.shape[1]
        squares = jnp.sum(middle * middle, axis=1, keepdims=True)
        lane = lax.broadcasted_iota(jnp.int32, (rows, sent_ref.shape[1] - width), 1)
        tail = jnp.zeros(lane.shape, jnp.float32)
        for i, term in enumerate(three_terms(squares)):
            tail = jnp.where(lane == i, term, tail)
        sent_ref[:, :width] = (middle * out_gain_ref[...]).astype(jnp.bfloat16)
        sent_ref[:, width:] = tail.astype(jnp.bfloat16)
        rounded = middle.astype(jnp.bfloat16)
        halves_ref[0, :, :width] = rounded
        halves_ref[1, :, :width] = (middle - rounded.astype(jnp.float32)).astype(jnp.bfloat16)
        halves_ref[:, :, width:] = jnp.zeros((2,) + lane.shape, jnp.bfloat16)


def split_kernel(grads_ref, out_ref, sems):
    quarter = out_ref.shape[3]
    copies = [
        pltpu.make_async_copy(
            grads_ref.at[:, :, pl.ds(k * quarter, quarter)], out_ref.at[k], sems.at[k]
        )
        for k in range(out_ref.shape[0])
    ]
    for copy in copies:
        copy.start()
    for copy in copies:
        copy.wait()


def adam_kernel(grads_ref, w_ref, m1_ref, m2_ref, new_ref, blocks_ref, grad_ref):
    members, _, double = blocks_ref.shape
    width = double // 2
    for i in range(members // 2):
        cut = slice(i * double, (i + 1) * double)
        total = grads_ref[0, :, :, cut].astype(jnp.float32)
        for shard in range(1, grads_ref.shape[0]):
            total = total + grads_ref[shard, :, :, cut].astype(jnp.float32)
        grad_ref[:, :, cut] = total
    for half in range(2):
        for i in range(members // 2):
            cut = slice(i * double, (i + 1) * double)
            grad_sum = grad_ref[:, half, cut]
            new = adam_update(
                grad_sum, w_ref[:, half, cut], m1_ref[:, half, cut], m2_ref[:, half, cut]
            )
            new_ref[:, half, cut] = new
            place = slice(half * width, (half + 1) * width)
            blocks_ref[2 * i, :, place] = new[:, :width].astype(jnp.bfloat16)
            blocks_ref[2 * i + 1, :, place] = new[:, width:].astype(jnp.bfloat16)


def up_kernel(x_ref, slab_ref, out_ref):
    copies, height, units = out_ref.shape
    rows = x_ref.shape[1]
    bands, width = slab_ref.shape[0], slab_ref.shape[3] // 2
    total = jnp.zeros((rows, units), jnp.float32)
    squares = jnp.zeros((rows, 1), jnp.float32)
    for band in range(bands):
        x = x_ref[band]
        total += lax.dot_general(
            x[:, :width],
            slab_ref[band, :, :, :width].reshape(units, width),
            (((1,), (1,)), ((), ())),
            preferred_element_type=jnp.float32,
        )
        squares += jnp.sum(x[:, width:].astype(jnp.float32), axis=1, keepdims=True)
    line = to_lanes(squares, units)
    row = lax.broadcasted_iota(jnp.int32, (height - rows, units), 0)
    tail = jnp.zeros((height - rows, units), jnp.float32)
    for i, term in enumerate(three_terms(line)):
        tail = jnp.where(row == i, term, tail)
    total = total.astype(out_ref.dtype)
    tail = tail.astype(out_ref.dtype)
    for copy in range(copies):
        out_ref[copy, :rows] = total
        out_ref[copy, rows:] = tail


def down_kernel(sums_ref, slab_ref, out_ref):
    bands, half, double = out_ref.shape
    rows, width = 2 * half, double // 2
    total = jnp.sum(sums_ref[...].astype(jnp.float32), axis=0)
    squares = jnp.sum(total[rows : rows + 8], axis=0, keepdims=True)
    factor = lax.rsqrt(to_rows(squares, rows) / D + norm_eps)
    upper = jnp.maximum(total[:rows] * factor, 0.0)
    active = (upper * upper).astype(jnp.bfloat16)
    for band in range(bands):
        weights = slab_ref[band, :, :, width:].reshape(active.shape[1], width)
        part = jnp.dot(active, weights, preferred_element_type=jnp.float32).astype(out_ref.dtype)
        out_ref[band, :, :width] = part[:half]
        out_ref[band, :, width:] = part[half:]


def finish_kernel(parts_ref, x_ref, out_ref):
    bands, half, double = parts_ref.shape
    width = double // 2
    steps = out_ref.shape[1]
    total = jnp.sum(parts_ref[...].astype(jnp.float32), axis=0)
    middle = jnp.sum(x_ref[bands:, :, :width].astype(jnp.float32), axis=0)
    for side in range(2):
        rows = slice(side * half, (side + 1) * half)
        done = middle[rows] + total[:, side * width : (side + 1) * width]
        count = half // steps
        out_ref[side * count : (side + 1) * count] = done.reshape(count, steps, width).astype(
            out_ref.dtype
        )


VMEM = pl.BlockSpec(memory_space=pltpu.VMEM)
SMEM = pl.BlockSpec(memory_space=pltpu.SMEM)


def whole(shape):
    return pl.BlockSpec(shape, lambda i: (0,) * len(shape))


def attend(lengths, hidden, squares, gain, out_gain, kv):
    rows, width = hidden.shape
    count = kv.shape[0]
    groups = width // HEAD
    pairs = 2
    block = (2 * pairs,) + kv.shape[1:]
    return pl.pallas_call(
        functools.partial(attend_kernel, pairs),
        grid=(count // (2 * pairs),),
        out_shape=(
            jax.ShapeDtypeStruct((rows, 640), jnp.bfloat16),
            jax.ShapeDtypeStruct((2, rows, 640), jnp.bfloat16),
        ),
        in_specs=[
            SMEM,
            whole(hidden.shape),
            whole(squares.shape),
            whole(gain.shape),
            whole(out_gain.shape),
            pl.BlockSpec(block, lambda i: (i, 0, 0)),
        ],
        out_specs=(whole((rows, 640)), whole((2, rows, 640))),
        scratch_shapes=[
            pltpu.VMEM((rows, width), jnp.float32),
            pltpu.VMEM((groups, rows, HEAD), jnp.float32),
            pltpu.VMEM((groups, rows, HEAD), jnp.float32),
            pltpu.VMEM((rows, HEAD), jnp.float32),
        ],
        compiler_params=pltpu.CompilerParams(vmem_limit_bytes=24 * 1024 * 1024),
    )(lengths, hidden, squares, gain, out_gain, kv)


def body(grad_parts, master, moment1, moment2, kv_cache, hidden_in, attn_gain, ffn_gain, lengths):
    role_index = lax.axis_index("role")
    shards = lax.axis_size("dp")
    tensor = lax.axis_size("tensor")
    bands = tensor // BAND
    bf16 = jnp.bfloat16
    band_groups = [[b * BAND + m for m in range(BAND)] for b in range(bands)]
    member_groups = [[b * BAND + m for b in range(bands)] for m in range(BAND)]
    quarter = master.shape[3]

    grads = grad_parts[0, 0]
    row_count, steps, width = hidden_in.shape
    rows = row_count * steps
    units = master.shape[1]
    wide = 640

    def learn():
        split = pl.pallas_call(
            split_kernel,
            out_shape=jax.ShapeDtypeStruct((shards, units, 2, quarter), bf16),
            in_specs=[pl.BlockSpec(memory_space=pl.ANY)],
            out_specs=VMEM,
            scratch_shapes=[pltpu.SemaphoreType.DMA((shards,))],
            compiler_params=pltpu.CompilerParams(vmem_limit_bytes=16 * 1024 * 1024),
        )(grads)
        arriving = lax.all_to_all(split, "dp", 0, 0, tiled=True)
        new_master, blocks = pl.pallas_call(
            adam_kernel,
            out_shape=(
                jax.ShapeDtypeStruct((units, 2, quarter), jnp.float32),
                jax.ShapeDtypeStruct((BAND, units, 2 * width), bf16),
            ),
            in_specs=[VMEM] * 4,
            out_specs=(VMEM, VMEM),
            scratch_shapes=[pltpu.VMEM((units, 2, quarter), jnp.float32)],
            compiler_params=pltpu.CompilerParams(vmem_limit_bytes=24 * 1024 * 1024),
        )(arriving, master[0], moment1[0], moment2[0])
        own = lax.all_to_all(blocks, "tensor", 0, 0, tiled=True, axis_index_groups=band_groups)
        return (
            new_master,
            own,
            jnp.zeros((bands + 2, rows, wide), bf16),
        )

    def roll_out():
        squares = pl.pallas_call(
            squares_kernel,
            out_shape=jax.ShapeDtypeStruct((tensor, 8, 128), jnp.float32),
            in_specs=[VMEM],
            out_specs=VMEM,
            compiler_params=pltpu.CompilerParams(vmem_limit_bytes=16 * 1024 * 1024),
        )(hidden_in)
        squares = lax.all_to_all(squares, "tensor", 0, 0, tiled=True)
        hidden = hidden_in.astype(jnp.float32).reshape(rows, width)
        feature_start = lax.axis_index("tensor") * width
        outgoing, halves = attend(
            lengths,
            hidden,
            squares,
            lax.dynamic_slice_in_dim(attn_gain, feature_start, width)[None],
            lax.dynamic_slice_in_dim(ffn_gain, feature_start, width)[None],
            kv_cache[0, :, 0],
        )
        features = lax.all_to_all(
            jnp.broadcast_to(outgoing[None], (bands, rows, wide)),
            "tensor",
            0,
            0,
            tiled=True,
            axis_index_groups=member_groups,
        )
        return (
            jnp.zeros((units, 2, quarter), jnp.float32),
            jnp.zeros((BAND, units, 2 * width), bf16),
            jnp.concatenate([features, halves]),
        )

    new_master, own, features = lax.cond(role_index == 0, learn, roll_out)
    features = lax.ppermute(features, "role", [(1, 0)])

    def gather_slabs():
        return lax.all_to_all(
            jnp.broadcast_to(own[None], (shards,) + own.shape), "dp", 0, 0, tiled=True
        )

    def no_slabs():
        return jnp.zeros((shards,) + own.shape, bf16)

    slabs = lax.cond(role_index == 0, gather_slabs, no_slabs)
    sums = pl.pallas_call(
        up_kernel,
        out_shape=jax.ShapeDtypeStruct((BAND, rows + 16, BAND * units), bf16),
        in_specs=[VMEM, VMEM],
        out_specs=VMEM,
        compiler_params=pltpu.CompilerParams(vmem_limit_bytes=16 * 1024 * 1024),
    )(features, slabs)
    sums = lax.all_to_all(sums, "tensor", 0, 0, tiled=True, axis_index_groups=band_groups)
    sums, new_master = lax.optimization_barrier((sums, new_master))
    copied = lax.ppermute(new_master, "role", [(0, 1)]).astype(bf16).astype(jnp.float32)
    weights_after = jnp.where(role_index == 0, new_master, copied)[None]
    parts = pl.pallas_call(
        down_kernel,
        out_shape=jax.ShapeDtypeStruct((bands, rows // 2, 2 * width), bf16),
        in_specs=[VMEM, VMEM],
        out_specs=VMEM,
        compiler_params=pltpu.CompilerParams(vmem_limit_bytes=16 * 1024 * 1024),
    )(sums, slabs)
    parts = lax.all_to_all(parts, "tensor", 0, 0, tiled=True, axis_index_groups=member_groups)
    decoded = pl.pallas_call(
        finish_kernel,
        out_shape=jax.ShapeDtypeStruct((row_count, steps, width), bf16),
        in_specs=[VMEM, VMEM],
        out_specs=VMEM,
        compiler_params=pltpu.CompilerParams(vmem_limit_bytes=16 * 1024 * 1024),
    )(parts, features)
    returned = lax.ppermute(decoded, "role", [(0, 1)])
    return (weights_after, jnp.where(role_index == 0, decoded, returned))


def solution(mesh):
    in_specs = (
        P("role", "dp", "tensor", None, None),
        P("role", "tensor", None, "dp"),
        P("role", "tensor", None, "dp"),
        P("role", "tensor", None, "dp"),
        P("role", "dp", "tensor", None, None),
        P("dp", None, "tensor"),
        P(),
        P(),
        P("dp"),
    )
    out_specs = (P("role", "tensor", None, "dp"), P("dp", None, "tensor"))
    return jax.shard_map(body, mesh=mesh, in_specs=in_specs, out_specs=out_specs, check_vma=False)
```

```python
import functools
import math

import jax
import jax.numpy as jnp
from jax import lax
from jax.experimental import pallas as pl
from jax.experimental.pallas import tpu as pltpu
from jax.sharding import PartitionSpec as P

D = 18432
HEAD = 192
STEPS = 4
BAND = 8


beta_one = 0.9
beta_two = 0.95
rate_factor = 0.5
decay_rate = 0.1
adam_eps = 1e-08
norm_eps = 1e-05
step_count = 10


def adam_update(grad_sum, weights, first, second):
    learn_rate = rate_factor / math.sqrt(D)
    first_new = beta_one * first + (1.0 - beta_one) * grad_sum
    second_new = beta_two * second + (1.0 - beta_two) * grad_sum * grad_sum
    corr_one = 1.0 - beta_one**step_count
    corr_two = 1.0 - beta_two**step_count
    ratio = first_new / corr_one / (jnp.sqrt(second_new / corr_two) + adam_eps)
    return weights - learn_rate * (ratio + decay_rate * weights)


def to_lanes(column, lanes):
    rows = column.shape[0]
    here = lax.broadcasted_iota(jnp.int32, (rows, lanes), 0)
    lane = lax.broadcasted_iota(jnp.int32, (rows, lanes), 1)
    return jnp.sum(jnp.where(here == lane, column, 0.0), axis=0, keepdims=True)


def to_rows(line, rows):
    lanes = line.shape[1]
    here = lax.broadcasted_iota(jnp.int32, (rows, lanes), 0)
    lane = lax.broadcasted_iota(jnp.int32, (rows, lanes), 1)
    return jnp.sum(jnp.where(here == lane, line, 0.0), axis=1, keepdims=True)


def three_terms(values):
    high = values.astype(jnp.bfloat16).astype(jnp.float32)
    middle = (values - high).astype(jnp.bfloat16).astype(jnp.float32)
    return high, middle, values - high - middle


def squares_kernel(hidden_ref, out_ref):
    hidden = hidden_ref[...].astype(jnp.float32)
    squares = jnp.sum(hidden * hidden, axis=2, keepdims=True)
    shape = hidden.shape[:2] + (out_ref.shape[2],)
    row = lax.broadcasted_iota(jnp.int32, shape, 0) * shape[1]
    row = row + lax.broadcasted_iota(jnp.int32, shape, 1)
    lane = lax.broadcasted_iota(jnp.int32, shape, 2)
    line = jnp.sum(jnp.where(lane == row, squares, 0.0), axis=(0, 1))
    out_ref[...] = jnp.broadcast_to(line[None, None], out_ref.shape)


def attend_kernel(
    pairs,
    len_ref,
    hidden_ref,
    squares_ref,
    gain_ref,
    out_gain_ref,
    kv_ref,
    sent_ref,
    halves_ref,
    middle_ref,
    normed_ref,
    hidden_parts_ref,
    flip_normed_ref,
):
    step = pl.program_id(0)
    groups = normed_ref.shape[0]
    rows = hidden_ref.shape[0]
    scale = 1.0 / math.sqrt(HEAD)

    @pl.when(step == 0)
    def _():
        total = jnp.sum(squares_ref[...], axis=0)[0:1]
        factor = lax.rsqrt(to_rows(total, rows) / D + norm_eps)
        hidden = hidden_ref[...]
        normed = hidden * factor * gain_ref[...]
        for q in range(groups):
            part = slice(q * HEAD, (q + 1) * HEAD)
            normed_ref[q] = normed[:, part]
            hidden_parts_ref[q] = hidden[:, part]
        across = lax.broadcasted_iota(jnp.int32, (HEAD, HEAD), 0)
        down = lax.broadcasted_iota(jnp.int32, (HEAD, HEAD), 1)
        reverse = jnp.where(across + down == HEAD - 1, 1.0, 0.0).astype(jnp.bfloat16)
        flip_normed_ref[...] = jnp.dot(
            normed_ref[0].astype(jnp.bfloat16), reverse, preferred_element_type=jnp.float32
        )

    high = lax.broadcasted_iota(jnp.int32, (groups * 8, 1), 0) % 8 >= 4
    row_id = lax.broadcasted_iota(jnp.int32, (groups * 8, 8), 0) % 8
    col_id = lax.broadcasted_iota(jnp.int32, (groups * 8, 8), 1)
    fresh_ok = (row_id // 4 == col_id // 4) & (col_id % 4 <= row_id % 4)
    context = kv_ref.shape[1]
    position = lax.broadcasted_iota(jnp.int32, (groups * 8, context), 1)
    for p in range(pairs):
        pair = step * pairs + p
        first = pl.multiple_of(pair * 8, 8)
        query = jnp.concatenate(
            [normed_ref[q, pl.ds(first, 8), :] for q in range(groups)], axis=0
        ).astype(jnp.bfloat16)
        new_keys = flip_normed_ref[pl.ds(first, 8), :].astype(jnp.bfloat16)
        new_values = normed_ref[1, pl.ds(first, 8), :].astype(jnp.bfloat16)
        contract = (((1,), (1,)), ((), ()))
        scores = []
        for half in range(2):
            keys = kv_ref[2 * p + half, :, :HEAD]
            scores.append(
                lax.dot_general(query, keys, contract, preferred_element_type=jnp.float32)
            )
        cache = jnp.where(high, scores[1], scores[0]) * scale
        length = jnp.where(high, len_ref[2 * pair + 1], len_ref[2 * pair])
        cache = jnp.where(position < length, cache, -jnp.inf)
        fresh = (
            lax.dot_general(query, new_keys, contract, preferred_element_type=jnp.float32)
            * scale
        )
        fresh = jnp.where(fresh_ok, fresh, -jnp.inf)
        top = jnp.maximum(
            jnp.max(cache, axis=1, keepdims=True), jnp.max(fresh, axis=1, keepdims=True)
        )
        cache = jnp.exp(cache - top)
        fresh = jnp.exp(fresh - top)
        total = jnp.sum(cache, axis=1, keepdims=True) + jnp.sum(fresh, axis=1, keepdims=True)
        cache = (cache / total).astype(jnp.bfloat16)
        fresh = (fresh / total).astype(jnp.bfloat16)
        weighed = []
        for half in range(2):
            values = kv_ref[2 * p + half, :, HEAD:]
            weighed.append(jnp.dot(cache, values, preferred_element_type=jnp.float32))
        attended = jnp.where(high, weighed[1], weighed[0]) + jnp.dot(
            fresh, new_values, preferred_element_type=jnp.float32
        )
        for q in range(groups):
            middle_ref[pl.ds(first, 8), q * HEAD : (q + 1) * HEAD] = (
                hidden_parts_ref[q, pl.ds(first, 8), :] + attended[q * 8 : (q + 1) * 8]
            )

    @pl.when(step == pl.num_programs(0) - 1)
    def _():
        middle = middle_ref[...]
        width = middle.shape[1]
        squares = jnp.sum(middle * middle, axis=1, keepdims=True)
        lane = lax.broadcasted_iota(jnp.int32, (rows, sent_ref.shape[1] - width), 1)
        tail = jnp.zeros(lane.shape, jnp.float32)
        for i, term in enumerate(three_terms(squares)):
            tail = jnp.where(lane == i, term, tail)
        sent_ref[:, :width] = (middle * out_gain_ref[...]).astype(jnp.bfloat16)
        sent_ref[:, width:] = tail.astype(jnp.bfloat16)
        rounded = middle.astype(jnp.bfloat16)
        halves_ref[0, :, :width] = rounded
        halves_ref[1, :, :width] = (middle - rounded.astype(jnp.float32)).astype(jnp.bfloat16)
        halves_ref[:, :, width:] = jnp.zeros((2,) + lane.shape, jnp.bfloat16)


def split_kernel(grads_ref, out_ref, blank_ref, sems):
    quarter = out_ref.shape[3]
    copies = [
        pltpu.make_async_copy(
            grads_ref.at[:, :, pl.ds(k * quarter, quarter)], out_ref.at[k], sems.at[k]
        )
        for k in range(out_ref.shape[0])
    ]
    for copy in copies:
        copy.start()
    del blank_ref
    for copy in copies:
        copy.wait()


def adam_kernel(grads_ref, w_ref, m1_ref, m2_ref, new_ref, blocks_ref, grad_ref):
    members, _, double = blocks_ref.shape
    width = double // 2
    for i in range(members // 2):
        cut = slice(i * double, (i + 1) * double)
        total = grads_ref[0, :, :, cut].astype(jnp.float32)
        for shard in range(1, grads_ref.shape[0]):
            total = total + grads_ref[shard, :, :, cut].astype(jnp.float32)
        grad_ref[:, :, cut] = total
    for half in range(2):
        for i in range(members // 2):
            cut = slice(i * double, (i + 1) * double)
            grad_sum = grad_ref[:, half, cut]
            new = adam_update(
                grad_sum, w_ref[:, half, cut], m1_ref[:, half, cut], m2_ref[:, half, cut]
            )
            new_ref[:, half, cut] = new
            place = slice(half * width, (half + 1) * width)
            blocks_ref[2 * i, :, place] = new[:, :width].astype(jnp.bfloat16)
            blocks_ref[2 * i + 1, :, place] = new[:, width:].astype(jnp.bfloat16)


def up_kernel(x_ref, slab_ref, out_ref):
    copies, height, units = out_ref.shape
    rows = x_ref.shape[1]
    bands, width = slab_ref.shape[0], slab_ref.shape[3] // 2
    total = jnp.zeros((rows, units), jnp.float32)
    squares = jnp.zeros((rows, 1), jnp.float32)
    for band in range(bands):
        x = x_ref[band]
        total += lax.dot_general(
            x[:, :width],
            slab_ref[band, :, :, :width].reshape(units, width),
            (((1,), (1,)), ((), ())),
            preferred_element_type=jnp.float32,
        )
        squares += jnp.sum(x[:, width:].astype(jnp.float32), axis=1, keepdims=True)
    line = to_lanes(squares, units)
    row = lax.broadcasted_iota(jnp.int32, (height - rows, units), 0)
    tail = jnp.zeros((height - rows, units), jnp.float32)
    for i, term in enumerate(three_terms(line)):
        tail = jnp.where(row == i, term, tail)
    total = total.astype(out_ref.dtype)
    tail = tail.astype(out_ref.dtype)
    for copy in range(copies):
        out_ref[copy, :rows] = total
        out_ref[copy, rows:] = tail


def down_kernel(sums_ref, slab_ref, out_ref):
    bands, half, double = out_ref.shape
    rows, width = 2 * half, double // 2
    total = jnp.sum(sums_ref[...].astype(jnp.float32), axis=0)
    squares = jnp.sum(total[rows : rows + 8], axis=0, keepdims=True)
    factor = lax.rsqrt(to_rows(squares, rows) / D + norm_eps)
    upper = jnp.maximum(total[:rows] * factor, 0.0)
    active = (upper * upper).astype(jnp.bfloat16)
    for band in range(bands):
        weights = slab_ref[band, :, :, width:].reshape(active.shape[1], width)
        part = jnp.dot(active, weights, preferred_element_type=jnp.float32).astype(out_ref.dtype)
        out_ref[band, :, :width] = part[:half]
        out_ref[band, :, width:] = part[half:]


def finish_kernel(parts_ref, x_ref, out_ref):
    bands, half, double = parts_ref.shape
    width = double // 2
    steps = out_ref.shape[1]
    total = jnp.sum(parts_ref[...].astype(jnp.float32), axis=0)
    middle = jnp.sum(x_ref[bands:, :, :width].astype(jnp.float32), axis=0)
    for side in range(2):
        rows = slice(side * half, (side + 1) * half)
        done = middle[rows] + total[:, side * width : (side + 1) * width]
        count = half // steps
        out_ref[side * count : (side + 1) * count] = done.reshape(count, steps, width).astype(
            out_ref.dtype
        )


VMEM = pl.BlockSpec(memory_space=pltpu.VMEM)
SMEM = pl.BlockSpec(memory_space=pltpu.SMEM)


def whole(shape):
    return pl.BlockSpec(shape, lambda i: (0,) * len(shape))


def attend(lengths, hidden, squares, gain, out_gain, kv):
    rows, width = hidden.shape
    count = kv.shape[0]
    groups = width // HEAD
    pairs = 2
    block = (2 * pairs,) + kv.shape[1:]
    return pl.pallas_call(
        functools.partial(attend_kernel, pairs),
        grid=(count // (2 * pairs),),
        out_shape=(
            jax.ShapeDtypeStruct((rows, 640), jnp.bfloat16),
            jax.ShapeDtypeStruct((2, rows, 640), jnp.bfloat16),
        ),
        in_specs=[
            SMEM,
            whole(hidden.shape),
            whole(squares.shape),
            whole(gain.shape),
            whole(out_gain.shape),
            pl.BlockSpec(block, lambda i: (i, 0, 0)),
        ],
        out_specs=(whole((rows, 640)), whole((2, rows, 640))),
        scratch_shapes=[
            pltpu.VMEM((rows, width), jnp.float32),
            pltpu.VMEM((groups, rows, HEAD), jnp.float32),
            pltpu.VMEM((groups, rows, HEAD), jnp.float32),
            pltpu.VMEM((rows, HEAD), jnp.float32),
        ],
        compiler_params=pltpu.CompilerParams(vmem_limit_bytes=24 * 1024 * 1024),
    )(lengths, hidden, squares, gain, out_gain, kv)


def body(grad_parts, master, moment1, moment2, kv_cache, hidden_in, attn_gain, ffn_gain, lengths):
    role_index = lax.axis_index("role")
    shards = lax.axis_size("dp")
    tensor = lax.axis_size("tensor")
    bands = tensor // BAND
    bf16 = jnp.bfloat16
    band_groups = [[b * BAND + m for m in range(BAND)] for b in range(bands)]
    member_groups = [[b * BAND + m for b in range(bands)] for m in range(BAND)]
    quarter = master.shape[3]

    grads = grad_parts[0, 0]
    row_count, steps, width = hidden_in.shape
    rows = row_count * steps
    units = master.shape[1]
    wide = 640

    def learn():
        split, blank = pl.pallas_call(
            split_kernel,
            out_shape=(
                jax.ShapeDtypeStruct((shards, units, 2, quarter), bf16),
                jax.ShapeDtypeStruct((bands + 2, rows, wide), bf16),
            ),
            in_specs=[pl.BlockSpec(memory_space=pl.ANY)],
            out_specs=(VMEM, pl.BlockSpec(memory_space=pl.ANY)),
            scratch_shapes=[pltpu.SemaphoreType.DMA((shards,))],
            compiler_params=pltpu.CompilerParams(vmem_limit_bytes=16 * 1024 * 1024),
        )(grads)
        arriving = lax.all_to_all(split, "dp", 0, 0, tiled=True)
        new_master, blocks = pl.pallas_call(
            adam_kernel,
            out_shape=(
                jax.ShapeDtypeStruct((units, 2, quarter), jnp.float32),
                jax.ShapeDtypeStruct((BAND, units, 2 * width), bf16),
            ),
            in_specs=[VMEM] * 4,
            out_specs=(VMEM, VMEM),
            scratch_shapes=[pltpu.VMEM((units, 2, quarter), jnp.float32)],
            compiler_params=pltpu.CompilerParams(vmem_limit_bytes=24 * 1024 * 1024),
        )(arriving, master[0], moment1[0], moment2[0])
        own = lax.all_to_all(blocks, "tensor", 0, 0, tiled=True, axis_index_groups=band_groups)
        return (
            new_master,
            own,
            blank,
        )

    def roll_out():
        squares = pl.pallas_call(
            squares_kernel,
            out_shape=jax.ShapeDtypeStruct((tensor, 8, 128), jnp.float32),
            in_specs=[VMEM],
            out_specs=VMEM,
            compiler_params=pltpu.CompilerParams(vmem_limit_bytes=16 * 1024 * 1024),
        )(hidden_in)
        squares = lax.all_to_all(squares, "tensor", 0, 0, tiled=True)
        hidden = hidden_in.astype(jnp.float32).reshape(rows, width)
        feature_start = lax.axis_index("tensor") * width
        outgoing, halves = attend(
            lengths,
            hidden,
            squares,
            lax.dynamic_slice_in_dim(attn_gain, feature_start, width)[None],
            lax.dynamic_slice_in_dim(ffn_gain, feature_start, width)[None],
            kv_cache[0, :, 0],
        )
        features = lax.all_to_all(
            jnp.broadcast_to(outgoing[None], (bands, rows, wide)),
            "tensor",
            0,
            0,
            tiled=True,
            axis_index_groups=member_groups,
        )
        return (
            jnp.zeros((units, 2, quarter), jnp.float32),
            jnp.zeros((BAND, units, 2 * width), bf16),
            jnp.concatenate([features, halves]),
        )

    new_master, own, features = lax.cond(role_index == 0, learn, roll_out)
    features = lax.ppermute(features, "role", [(1, 0)])

    def gather_slabs():
        return lax.all_to_all(
            jnp.broadcast_to(own[None], (shards,) + own.shape), "dp", 0, 0, tiled=True
        )

    def no_slabs():
        return jnp.zeros((shards,) + own.shape, bf16)

    slabs = lax.cond(role_index == 0, gather_slabs, no_slabs)
    sums = pl.pallas_call(
        up_kernel,
        out_shape=jax.ShapeDtypeStruct((BAND, rows + 16, BAND * units), bf16),
        in_specs=[VMEM, VMEM],
        out_specs=VMEM,
        compiler_params=pltpu.CompilerParams(vmem_limit_bytes=16 * 1024 * 1024),
    )(features, slabs)
    sums = lax.all_to_all(sums, "tensor", 0, 0, tiled=True, axis_index_groups=band_groups)
    sums, new_master = lax.optimization_barrier((sums, new_master))
    copied = lax.ppermute(new_master, "role", [(0, 1)]).astype(bf16).astype(jnp.float32)
    weights_after = jnp.where(role_index == 0, new_master, copied)[None]
    parts = pl.pallas_call(
        down_kernel,
        out_shape=jax.ShapeDtypeStruct((bands, rows // 2, 2 * width), bf16),
        in_specs=[VMEM, VMEM],
        out_specs=VMEM,
        compiler_params=pltpu.CompilerParams(vmem_limit_bytes=16 * 1024 * 1024),
    )(sums, slabs)
    parts = lax.all_to_all(parts, "tensor", 0, 0, tiled=True, axis_index_groups=member_groups)
    decoded = pl.pallas_call(
        finish_kernel,
        out_shape=jax.ShapeDtypeStruct((row_count, steps, width), bf16),
        in_specs=[VMEM, VMEM],
        out_specs=VMEM,
        compiler_params=pltpu.CompilerParams(vmem_limit_bytes=16 * 1024 * 1024),
    )(parts, features)
    returned = lax.ppermute(decoded, "role", [(0, 1)])
    return (weights_after, jnp.where(role_index == 0, decoded, returned))


def solution(mesh):
    in_specs = (
        P("role", "dp", "tensor", None, None),
        P("role", "tensor", None, "dp"),
        P("role", "tensor", None, "dp"),
        P("role", "tensor", None, "dp"),
        P("role", "dp", "tensor", None, None),
        P("dp", None, "tensor"),
        P(),
        P(),
        P("dp"),
    )
    out_specs = (P("role", "tensor", None, "dp"), P("dp", None, "tensor"))
    return jax.shard_map(body, mesh=mesh, in_specs=in_specs, out_specs=out_specs, check_vma=False)
```
